512 devices in a mesh: dp: 32 (over z, core), section: 8 (over x_hi, y), mp: 2 (over x_lo).
Axes of the slice: x: 4 (x_hi: 2, x_lo: 2; x = x_hi * 2 + x_lo), y: 4, z: 16, core: 2. Of those that a mesh axis runs over, the one named last changes fastest.
Arguments:
- neighbour_ids: int32 [64, 256], P('dp'), may hold values from 0 to 63999, as said below
- embed_table: bfloat16 [64000, 896], P(('dp', 'mp')), may hold values from -200 to 200
- enc_gain: float32 [896], replicated, may hold values from 0.1 to 1.9
- kv_weight: bfloat16 [8, 896, 2, 2048], P('section', 'dp', None, 'mp'), may hold values from -0.1875 to 0.1875
- queries: bfloat16 [8, 4096, 2048], P('section', 'dp', 'mp'), may hold values from -70 to 70
- grad_out: bfloat16 [8, 4096, 2048], P('section', 'dp', 'mp'), may hold values from -6 to 6
Outputs:
- attn_out: bfloat16 [8, 4096, 2048], P('section', 'dp', 'mp')
- grad_queries: bfloat16 [8, 4096, 2048], P('section', 'dp', 'mp')
- grad_kv_weight: bfloat16 [8, 896, 2, 2048], P('section', 'dp', None, 'mp')
- grad_encodings: bfloat16 [64, 256, 896], P('dp')
The draws below stay inside these ranges and needn't reach their ends.
Inputs may be any that keep to these rules, and one draw needn't show every extreme that they name: `neighbour_ids`: the ids of the 2 rows of one index of dp fall at most 12 times into one block of 1000 consecutive ids, and some block receives exactly 12 of them.
All inputs are finite; a program needn't handle non-finite values.
Results may differ from the reference program's by a relative error of at most 0.03.
The reference program's roundings to bfloat16 on the way count: a program that leaves them out, or rounds other values in their place, can miss the bound.
Values may be sent and summed in bfloat16 or wider, within the bound.
A program may use at most 64 MiB of HBM per device.

```python
import math
import jax
import jax.numpy as jnp
from jax import lax

ENC_WIDTH = 896
HEADS = 16
HEAD_DIM = 128
VOCAB = 64000
SPAN = 64
SPAN_DEV = 2
SECTIONS = 8
SPANS = 64
TOKENS = 4096
NBR_ROWS = 256
OWNERS = 64
OWNER_ROWS = 1000
CAPACITY = 12
N_DP = 32


def draw_neighbour_ids(key, part):
    key = jax.random.fold_in(key, 11)
    block_count = SPANS // SPAN_DEV
    block_rows = SPAN_DEV * NBR_ROWS
    slot_count = OWNERS * CAPACITY

    def one_block(block_index):
        block_key = jax.random.fold_in(key, block_index)
        key_perm, key_full, key_mix, key_offset = jax.random.split(block_key, 4)
        owner_list = jnp.arange(slot_count, dtype=jnp.int32) // CAPACITY
        rank_list = jax.random.permutation(key_perm, slot_count).astype(jnp.int32)
        chosen = jax.random.randint(key_full, (), 0, OWNERS, dtype=jnp.int32)
        rank_list = jnp.where(owner_list == chosen, rank_list - slot_count, rank_list)
        order_list = jnp.argsort(rank_list, stable=True)
        picked = owner_list[order_list[:block_rows]]
        picked = jax.random.permutation(key_mix, picked)
        offsets = jax.random.randint(key_offset, (block_rows,), 0, OWNER_ROWS, dtype=jnp.int32)
        return picked * OWNER_ROWS + offsets
    all_ids = jax.vmap(one_block)(jnp.arange(block_count, dtype=jnp.int32))
    return all_ids.reshape(SPANS, NBR_ROWS).astype(jnp.int32)


def draw_embed_table(key, part):
    key = jax.random.fold_in(key, 23)
    key_main, key_rows, key_cols = jax.random.split(key, 3)
    row_scale = jnp.exp(jax.random.uniform(key_rows, (VOCAB, 1), minval=0.0, maxval=math.log(10.0)))
    col_scale = jnp.exp(jax.random.uniform(key_cols, (1, ENC_WIDTH), minval=0.0, maxval=math.log(10.0)))
    base = jnp.clip(jax.random.normal(key_main, (VOCAB, ENC_WIDTH)), -6.0, 6.0)
    return (base * row_scale * col_scale / 3.0).astype(jnp.bfloat16)


def draw_queries(key, part):
    key = jax.random.fold_in(key, 37)
    key_main, key_rows = jax.random.split(key)
    full_shape = (SECTIONS, TOKENS, HEADS * HEAD_DIM)
    base = jnp.clip(jax.random.normal(key_main, full_shape), -6.0, 6.0)
    row_scale = jnp.exp(jax.random.uniform(key_rows, (SECTIONS, TOKENS, 1), minval=0.0, maxval=math.log(3.0)))
    return (base * row_scale).astype(jnp.bfloat16)


def levels(key, extent, cuts, smallest, top_value):
    def one(position, shards_of):
        heights = jax.random.uniform(jax.random.fold_in(jax.random.fold_in(key, 6), position), (shards_of,), jnp.float32, smallest / len(cuts), top_value / len(cuts))
        return jnp.repeat(jnp.exp(heights), extent[position] // shards_of).reshape((-1,) + (1,) * (len(extent) - position - 1))

    factor_of = one(*cuts[0])
    for cut in cuts[1:]:
        factor_of = factor_of * one(*cut)
    return factor_of


def scatter_about(stream_key, extent, deviation, limit, pieces=(), kind=jnp.bfloat16):
    drawn = jax.random.normal(stream_key, extent, jnp.float32) * deviation
    if len(pieces) > 0:
        drawn = levels(stream_key, extent, pieces, -0.22, 0.18) * drawn
    return jnp.clip(drawn, min=-limit, max=limit).astype(kind)


def setup_inputs(seed: int = 0) -> dict:
    streams_of = jax.random.split(jax.random.key(seed), 7)
    return {
        "neighbour_ids": draw_neighbour_ids(jax.random.fold_in(streams_of[6], 71), 0),
        "embed_table": draw_embed_table(jax.random.fold_in(streams_of[6], 71), 0),
        "enc_gain": jnp.clip(1.0 + 0.18 * jax.random.normal(streams_of[2], (ENC_WIDTH,), jnp.float32), 0.1, 1.9),
        "kv_weight": scatter_about(streams_of[3], (SECTIONS, ENC_WIDTH, 2, HEADS * HEAD_DIM), ENC_WIDTH ** -0.5, 0.1875, ((0, 8), (1, 32), (3, 2))),
        "queries": draw_queries(jax.random.fold_in(streams_of[6], 71), 0),
        "grad_out": scatter_about(streams_of[5], (SECTIONS, TOKENS, HEADS * HEAD_DIM), 1.0, 6.0, ((0, 8), (1, 32), (2, 2))),
    }


def encode_all(neighbour_ids, embed_table, enc_gain):
    looked = jnp.take(embed_table, neighbour_ids, axis=0).astype(jnp.float32)
    mean_square = lax.optimization_barrier(jnp.mean(looked * looked, axis=-1, keepdims=True))
    return (looked * lax.rsqrt(mean_square + 1e-06) * enc_gain).astype(jnp.bfloat16)

def reference(neighbour_ids, embed_table, enc_gain, kv_weight, queries, grad_out):
    encoded = encode_all(neighbour_ids, embed_table, enc_gain)
    enc_wide = encoded.astype(jnp.float32)
    span_count = encoded.shape[0]
    attn_width = HEADS * HEAD_DIM
    inv_root = 1.0 / math.sqrt(HEAD_DIM)
    grouped = enc_wide.reshape(N_DP, SPAN_DEV * NBR_ROWS, ENC_WIDTH)

    def add_group(summed, pair):
        enc_group, grad_group = pair
        partial_sum = jnp.einsum('re,rka->eka', enc_group, grad_group)
        partial_sum = lax.optimization_barrier(partial_sum.astype(jnp.bfloat16)).astype(jnp.float32)
        return (summed + partial_sum, None)

    def one_section(carry, inputs):
        weight, section_query, upstream = inputs
        weight_f = weight.astype(jnp.float32)
        keyval = jnp.einsum('cre,eka->crka', enc_wide, weight_f).astype(jnp.bfloat16)
        key_heads = keyval[:, :, 0].reshape(span_count, NBR_ROWS, HEADS, HEAD_DIM).astype(jnp.float32)
        value_heads = keyval[:, :, 1].reshape(span_count, NBR_ROWS, HEADS, HEAD_DIM).astype(jnp.float32)
        query_heads = section_query.reshape(span_count, SPAN, HEADS, HEAD_DIM).astype(jnp.float32)
        grad_heads = upstream.reshape(span_count, SPAN, HEADS, HEAD_DIM).astype(jnp.float32)
        scores = jnp.einsum('cqhd,crhd->chqr', query_heads, key_heads) * inv_root
        score_top = lax.optimization_barrier(jnp.max(scores, axis=-1, keepdims=True))
        expo_val = jnp.exp(scores - score_top)
        prob_f = expo_val / lax.optimization_barrier(jnp.sum(expo_val, axis=-1, keepdims=True))
        prob_b = prob_f.astype(jnp.bfloat16).astype(jnp.float32)
        attended = jnp.einsum('chqr,crhd->cqhd', prob_b, value_heads).astype(jnp.bfloat16)
        grad_prob = jnp.einsum('cqhd,crhd->chqr', grad_heads, value_heads)
        inner = lax.optimization_barrier(jnp.sum(grad_prob * prob_f, axis=-1, keepdims=True))
        grad_score = (prob_f * (grad_prob - inner) * inv_root).astype(jnp.bfloat16).astype(jnp.float32)
        grad_query = jnp.einsum('chqr,crhd->cqhd', grad_score, key_heads).astype(jnp.bfloat16)
        grad_key = jnp.einsum('chqr,cqhd->crhd', grad_score, query_heads).astype(jnp.bfloat16)
        grad_value = jnp.einsum('chqr,cqhd->crhd', prob_b, grad_heads).astype(jnp.bfloat16)
        grad_kv = jnp.stack([grad_key.reshape(span_count, NBR_ROWS, attn_width), grad_value.reshape(span_count, NBR_ROWS, attn_width)], axis=2).astype(jnp.float32)
        grad_grouped = grad_kv.reshape(N_DP, SPAN_DEV * NBR_ROWS, 2, attn_width)
        start_sum = jnp.zeros((ENC_WIDTH, 2, attn_width), jnp.float32)
        weight_sum, unused = lax.scan(add_group, start_sum, (grouped, grad_grouped))
        enc_term = jnp.einsum('crka,eka->cre', grad_kv, weight_f)
        outputs = (attended.reshape(TOKENS, attn_width), grad_query.reshape(TOKENS, attn_width), weight_sum.astype(jnp.bfloat16))
        return (carry + enc_term, outputs)
    start_enc = jnp.zeros(encoded.shape, jnp.float32)
    summed, stacked = lax.scan(one_section, start_enc, (kv_weight, queries, grad_out))
    attn_all, query_all, weight_all = stacked
    return (attn_all, query_all, weight_all, summed.astype(jnp.bfloat16))
```

```python
import functools
import math

import jax
import jax.numpy as jnp
from jax import lax
from jax.experimental import pallas as pl
from jax.experimental.pallas import tpu as pltpu
from jax.sharding import PartitionSpec as P

HEAD_DIM = 128
SPAN = 64
PACK = 16
MESH = pl.DeviceIdType.MESH
F32 = jnp.float32
BF16 = jnp.bfloat16
NT = (((1,), (1,)), ((), ()))
TN = (((0,), (0,)), ((), ()))


def dot(a, b, dims=(((1,), (0,)), ((), ()))):
    return lax.dot_general(a, b, dims, preferred_element_type=F32)


def iota(shape, axis):
    return lax.broadcasted_iota(jnp.int32, shape, axis)


def kernel(
    n_dp, n_sec, n_mp, cap, e_rows,
    ids_ref, table_ref, gain_ref, w_ref, q_ref, g_ref,
    attn_ref, gq_ref, wg_ref, genc_ref,
    ids_buf, pack_buf, land_buf, rows_buf, spread, pad_mat, place,
    enc_buf, enct_buf, wbuf, gbuf, eacc, pbuf, sib, sbuf, rbuf,
    esend, eland, gall,
    ids_send, ids_recv, pack_send, pack_recv, row_send, row_recv,
    ring_send, ring_recv, twin_send, twin_recv,
    half_send, half_recv, sum_send, sum_recv,
    part_send, part_recv, full_send, full_recv,
):
    nz = n_dp // 2
    n_plane = n_sec * n_mp
    n_tgt = n_dp // n_sec
    heads = wbuf.shape[0]
    nq = 4 if heads % 4 == 0 else 1
    hq = heads // nq
    half = nz * 32
    n_ids = ids_ref.shape[1]
    owner_rows = table_ref.shape[0]
    spans = q_ref.shape[0] // SPAN
    nbr = n_ids // spans
    out_rows = n_ids // n_plane
    k_long = nz // 2
    k_short = nz - 1 - k_long
    inv_root = 1.0 / math.sqrt(HEAD_DIM)

    me = lax.axis_index("dp")
    sec = lax.axis_index("section")
    mp = lax.axis_index("mp")
    z = me // 2
    core = lax.rem(me, 2)
    twin = 2 * z + (1 - core)
    here = sec * n_mp + mp
    asks = lax.rem(me, n_sec) == sec
    my_tgt = me // n_sec
    my_lane = lax.rem(me, n_sec)

    def up(step):
        return lax.rem(z + step + 2 * nz, nz)

    nexts = (2 * up(1) + core, 2 * up(-1) + core)

    def peer(j):
        p = lax.rem(here + j, n_plane)
        return (me, p // n_mp, lax.rem(p, n_mp))

    def remote(src, dst, send, recv, device):
        return pltpu.make_async_remote_copy(
            src_ref=src, dst_ref=dst, send_sem=send, recv_sem=recv,
            device_id=device, device_id_type=MESH,
        )

    def drain(ref, sem):
        pltpu.make_async_copy(ref, ref, sem).wait()

    barrier = pltpu.get_barrier_semaphore()

    def greet(device):
        pl.semaphore_signal(barrier, inc=1, device_id=device, device_id_type=MESH)

    greet((nexts[0], sec, mp))
    greet((nexts[1], sec, mp))
    greet((twin, sec, mp))

    @pl.loop(1, n_plane)
    def _(j):
        greet(peer(j))

    for k in range(n_tgt):
        other = sec + n_sec * k

        @pl.when(other != me)
        def _():
            greet((other, sec, mp))

        @pl.when(jnp.logical_or(other != me, my_lane != sec))
        def _():
            greet((other, my_lane, mp))

    expected = 3 + (n_plane - 1) + n_tgt
    expected = expected + jnp.where(asks, n_dp - 1 - 1, 0)
    pl.semaphore_wait(barrier, expected)

    def shard(src_z, parity, q):
        row = pl.multiple_of(parity * half + src_z * 32, 32)
        return wbuf.at[pl.ds(q * hq, hq), pl.ds(row, 32), :]

    def ring_copy(q, way, k, src_z):
        block = shard(src_z, core, q)
        return remote(block, block, ring_send, ring_recv.at[way, q, k], (nexts[way], sec, mp))

    def twin_copy(q, src_z):
        block = shard(src_z, core, q)
        return remote(block, block, twin_send, twin_recv.at[q], (twin, sec, mp))

    def last_step(q, way):
        return k_long if (q + way) % 2 == 0 else k_short

    own = pl.multiple_of(core * half + z * 32, 32)
    wbuf[:, pl.ds(own, 32), :] = w_ref[...]

    @pl.when(asks)
    def _():
        ids_buf[my_tgt] = ids_ref[...]

        @pl.loop(1, n_dp)
        def _(j):
            to = lax.rem(me + j, n_dp)
            remote(ids_ref, ids_buf.at[my_tgt], ids_send, ids_recv.at[my_tgt], (to, sec, mp)).start()

    for q in range(nq):
        for way in range(2):
            if last_step(q, way) > 0:
                ring_copy(q, way, 0, z).start()
        twin_copy(q, z).start()

    def gather_step(k, live, onward):
        for q in range(nq):
            for way in range(2):
                if not live(q, way):
                    continue
                src_z = up(-k) if way == 0 else up(k)
                ring_copy(q, way, k - 1, src_z).wait_recv()
                if onward(q, way):
                    ring_copy(q, way, k, src_z).start()
                twin_copy(q, src_z).start()

    def gather_steps(lo, hi):
        @pl.loop(lo, hi)
        def _(k):
            gather_step(k, lambda q, way: True, lambda q, way: True)

    def owner_of(ids):
        return ((ids.astype(F32) + 0.5) * (1.0 / owner_rows)).astype(jnp.int32)

    def base_of(ids):
        owner = owner_of(ids)
        dev = owner // n_mp
        slot = (lax.rem(dev, n_sec) * n_mp + lax.rem(owner, n_mp)) * (n_tgt * cap)
        return slot + (dev // n_sec) * cap

    ids = ids_ref[...]
    base_row = jnp.broadcast_to(base_of(ids).astype(F32), (n_ids, n_ids))
    row_no = iota((n_ids, n_ids), 0)
    col_no = iota((n_ids, n_ids), 1)
    base_col = jnp.sum(jnp.where(row_no == col_no, base_row, 0.0), axis=1, keepdims=True)
    same = jnp.logical_and(base_row == base_col, col_no < row_no)
    slot_col = jnp.sum(jnp.where(same, 1.0, 0.0), axis=1, keepdims=True)
    want = (base_col + slot_col).astype(jnp.int32)
    packed_rows = n_plane * n_tgt * cap
    place[...] = jnp.where(iota((n_ids, packed_rows), 1) == want, 1.0, 0.0).astype(BF16)

    wide = 2 * half
    enc_width = n_dp * e_rows
    pos = iota((wide, 1), 0)
    blk = pos // 32
    dev = 2 * lax.rem(blk, nz) + blk // nz
    inner = lax.rem(pos, 32)
    feature = jnp.where(inner < e_rows, dev * e_rows + inner, -1)
    pad_mat[...] = jnp.where(iota((wide, enc_width), 1) == feature, 1.0, 0.0).astype(BF16)

    first = max(1, min(2, k_short))
    second = max(first, min(4, k_short))
    gather_steps(1, first)

    for k in range(n_tgt):

        @pl.when(sec + n_sec * k != me)
        def _():
            drain(ids_buf.at[k], ids_recv.at[k])

    block_no = me * n_mp + mp
    upper = jnp.where(iota((n_ids, n_ids), 0) < iota((n_ids, n_ids), 1), 1.0, 0.0).astype(BF16)
    offs = jnp.concatenate(
        [jnp.broadcast_to(ids_buf[k], (PACK, n_ids)) for k in range(n_tgt)], axis=0
    ) - block_no * owner_rows
    mine = jnp.logical_and(offs >= 0, offs < owner_rows)
    slots = dot(jnp.where(mine, 1.0, 0.0).astype(BF16), upper)
    rank = lax.rem(iota((n_tgt * PACK, n_ids), 0), PACK).astype(F32)
    pick = jnp.logical_and(mine, slots == rank)
    wanted = jnp.sum(jnp.where(pick, offs.astype(F32) + 1.0, 0.0), axis=1, keepdims=True) - 1.0
    hot = jnp.where(
        iota((n_tgt * PACK, owner_rows), 1) == wanted.astype(jnp.int32), 1.0, 0.0
    ).astype(BF16)
    pack_buf[...] = dot(hot, table_ref[...]).astype(BF16).reshape(pack_buf.shape)

    for k in range(n_tgt):
        to = sec + n_sec * k
        away = jnp.logical_or(to != me, my_lane != sec)

        @pl.when(away)
        def _():
            remote(
                pack_buf.at[k], land_buf.at[my_tgt], pack_send.at[k], pack_recv.at[my_tgt],
                (to, my_lane, mp),
            ).start()

        @pl.when(jnp.logical_not(away))
        def _():
            land_buf[my_tgt] = pack_buf[k]

    gather_steps(first, second)

    for k in range(n_tgt):

        @pl.when(jnp.logical_or(sec + n_sec * k != me, my_lane != sec))
        def _():
            drain(land_buf.at[k], pack_recv.at[k])

    tight = n_tgt * cap
    row = iota((tight, n_tgt * PACK), 0)
    col = iota((tight, n_tgt * PACK), 1)
    squeeze = jnp.where((row // cap) * PACK + lax.rem(row, cap) == col, 1.0, 0.0).astype(BF16)
    landed = land_buf[...].reshape(n_tgt * PACK, enc_width)
    rows_buf[...] = dot(squeeze, landed).astype(BF16)
    spread[here] = rows_buf[...]

    @pl.loop(1, n_plane)
    def _(j):
        remote(rows_buf, spread.at[here], row_send, row_recv, peer(j)).start()

    gather_steps(second, k_short)
    if k_short >= 1:
        gather_step(k_short, lambda q, w: True, lambda q, w: last_step(q, w) > k_short)
    gather_step(k_long, lambda q, w: last_step(q, w) == k_long, lambda q, w: False)

    drain(spread.at[pl.ds(0, n_plane - 1)], row_recv)

    looked = dot(place[...], spread[...].reshape(packed_rows, enc_width))
    mean_square = jnp.mean(looked * looked, axis=-1, keepdims=True)
    encoded = (looked * lax.rsqrt(mean_square + 1e-06) * gain_ref[...]).astype(BF16)
    enc_buf[...] = dot(encoded, pad_mat[...], NT).astype(BF16)
    enct_buf[...] = dot(pad_mat[...], encoded, NT).astype(BF16)

    for q in range(nq):
        block = wbuf.at[pl.ds(q * hq, hq), pl.ds(pl.multiple_of((1 - core) * half, 32), half), :]
        drain(block, twin_recv.at[q])

    eacc[...] = jnp.zeros_like(eacc)

    @pl.loop(0, nq)
    def _(q):
        for hh in range(hq):
            h = q * hq + hh
            weight = wbuf[h]
            keyval = dot(enc_buf[...], weight).astype(BF16)
            lanes = pl.ds(pl.multiple_of(h * HEAD_DIM, HEAD_DIM), HEAD_DIM)
            for c in range(spans):
                keys = keyval[c * nbr:(c + 1) * nbr, :HEAD_DIM]
                values = keyval[c * nbr:(c + 1) * nbr, HEAD_DIM:]
                tokens = pl.ds(c * SPAN, SPAN)
                query = q_ref[tokens, lanes]
                grad = g_ref[tokens, lanes]
                scores = dot(query, keys, NT) * inv_root
                expo = jnp.exp(scores - jnp.max(scores, axis=-1, keepdims=True))
                prob = expo / jnp.sum(expo, axis=-1, keepdims=True)
                prob_b = prob.astype(BF16)
                attn_ref[tokens, lanes] = dot(prob_b, values).astype(BF16)
                grad_prob = dot(grad, values, NT)
                mixed = jnp.sum(grad_prob * prob, axis=-1, keepdims=True)
                grad_score = (prob * (grad_prob - mixed) * inv_root).astype(BF16)
                gq_ref[tokens, lanes] = dot(grad_score, keys).astype(BF16)
                rows = pl.ds(c * nbr, nbr)
                gbuf[h, rows, :HEAD_DIM] = dot(grad_score, query, TN).astype(BF16)
                gbuf[h, rows, HEAD_DIM:] = dot(prob_b, grad, TN).astype(BF16)
            eacc[...] += dot(gbuf[h], weight, NT)

    esend[...] = dot(eacc[...].astype(BF16), pad_mat[...]).astype(BF16)

    def out_slice(p):
        return pl.ds(pl.multiple_of(p * out_rows, out_rows), out_rows)

    eland[here] = esend[out_slice(here), :]

    @pl.loop(1, n_plane)
    def _(j):
        device = peer(j)
        p = device[1] * n_mp + device[2]
        remote(esend.at[out_slice(p), :], eland.at[here], part_send, part_recv, device).start()

    away_half = pl.ds(pl.multiple_of((1 - core) * half, 32), half)

    @pl.loop(0, heads)
    def _(h):
        pbuf[h] = dot(enct_buf[...], gbuf[h]).astype(BF16)
        remote(
            pbuf.at[h, away_half, :], sib.at[h], half_send, half_recv.at[h], (twin, sec, mp)
        ).start()

    def pair(q, dest_z):
        hs = pl.ds(q * hq, hq)
        a = pbuf[hs, pl.ds(pl.multiple_of(core * half + dest_z * 32, 32), 32), :]
        b = sib[hs, pl.ds(pl.multiple_of(dest_z * 32, 32), 32), :]
        return a.astype(F32) + b.astype(F32)

    def sum_copy(src, q, way, k):
        return remote(
            src, rbuf.at[way, k, pl.ds(q * hq, hq)], sum_send, sum_recv.at[way, q, k],
            (nexts[way], sec, mp),
        )

    def dest(way, steps):
        return up(steps) if way == 0 else up(-steps)

    for q in range(nq):
        for hh in range(hq):
            drain(sib.at[q * hq + hh], half_recv.at[q * hq + hh])
        for way in range(2):
            steps = last_step(q, way)
            if steps > 0:
                block = sbuf.at[way, pl.ds(q * hq, hq)]
                block[...] = pair(q, dest(way, steps)).astype(BF16)
                sum_copy(block, q, way, 0).start()

    def sum_step(k, live):
        for q in range(nq):
            for way in range(2):
                if not live(q, way):
                    continue
                block = rbuf.at[way, k - 1, pl.ds(q * hq, hq)]
                sum_copy(block, q, way, k - 1).wait_recv()
                total = block[...].astype(F32) + pair(q, dest(way, last_step(q, way) - k))
                block[...] = total.astype(BF16)
                sum_copy(block, q, way, k).start()

    middle = max(1, min(4, k_short))

    @pl.loop(1, middle)
    def _(k):
        sum_step(k, lambda q, w: True)

    drain(eland.at[pl.ds(0, n_plane - 1)], part_recv)
    mine_rows = jnp.sum(eland[...].astype(F32), axis=0).astype(BF16)
    gall[out_slice(here), :] = mine_rows

    @pl.loop(1, n_plane)
    def _(j):
        block = gall.at[out_slice(here), :]
        remote(block, block, full_send, full_recv, peer(j)).start()

    @pl.loop(middle, k_short)
    def _(k):
        sum_step(k, lambda q, w: True)

    if k_short >= 1:
        sum_step(k_short, lambda q, w: last_step(q, w) > k_short)

    for q in range(nq):
        total = pair(q, z)
        for way in range(2):
            steps = last_step(q, way)
            if steps > 0:
                block = rbuf.at[way, steps - 1, pl.ds(q * hq, hq)]
                sum_copy(block, q, way, steps - 1).wait_recv()
                total = total + block[...].astype(F32)
        wg_ref[pl.ds(q * hq, hq)] = total.astype(BF16)

    drain(gall.at[pl.ds(0, (n_plane - 1) * out_rows), :], full_recv)
    genc_ref[...] = gall[...]

    @pl.when(asks)
    def _():
        @pl.loop(1, n_dp)
        def _(j):
            drain(ids_ref, ids_send)

    for k in range(n_tgt):

        @pl.when(jnp.logical_or(sec + n_sec * k != me, my_lane != sec))
        def _():
            drain(pack_buf.at[k], pack_send.at[k])

    drain(spread.at[pl.ds(0, n_plane - 1)], row_send)
    sent = pl.ds(0, (nz - 1) * 32)
    drain(wbuf.at[:, sent, :], ring_send)
    drain(wbuf.at[:, pl.ds(0, half), :], twin_send)
    drain(sib, half_send)
    drain(sib.at[:, sent, :], sum_send)
    drain(eland.at[pl.ds(0, n_plane - 1)], part_send)
    drain(gall.at[pl.ds(0, (n_plane - 1) * out_rows), :], full_send)


def body(n_dp, n_sec, n_mp, neighbour_ids, embed_table, enc_gain, kv_weight, queries, grad_out):
    spans, nbr = neighbour_ids.shape
    n_ids = spans * nbr
    owner_rows, enc_width = embed_table.shape
    e_rows, local = kv_weight.shape[1], kv_weight.shape[3]
    heads = local // HEAD_DIM
    tokens = queries.shape[1]
    cap = 3 * n_ids // (2 * n_dp * n_mp)
    nz, n_plane, n_tgt = n_dp // 2, n_sec * n_mp, n_dp // n_sec
    half = nz * 32
    nq = 4 if heads % 4 == 0 else 1
    k_long = nz // 2
    weight = kv_weight[0].reshape(e_rows, 2, heads, HEAD_DIM).transpose(2, 0, 1, 3)
    weight = jnp.pad(weight.reshape(heads, e_rows, 2 * HEAD_DIM), ((0, 0), (0, 32 - e_rows), (0, 0)))
    vmem = pl.BlockSpec(memory_space=pltpu.VMEM)
    dma = pltpu.SemaphoreType.DMA
    out = pl.pallas_call(
        functools.partial(kernel, n_dp, n_sec, n_mp, cap, e_rows),
        out_shape=(
            jax.ShapeDtypeStruct((tokens, local), BF16),
            jax.ShapeDtypeStruct((tokens, local), BF16),
            jax.ShapeDtypeStruct((heads, 32, 2 * HEAD_DIM), BF16),
            jax.ShapeDtypeStruct((n_ids, enc_width), BF16),
        ),
        in_specs=[vmem] * 6,
        out_specs=(vmem,) * 4,
        scratch_shapes=[
            pltpu.VMEM((n_tgt, 1, n_ids), jnp.int32),
            pltpu.VMEM((n_tgt, PACK, enc_width), BF16),
            pltpu.VMEM((n_tgt, PACK, enc_width), BF16),
            pltpu.VMEM((n_tgt * cap, enc_width), BF16),
            pltpu.VMEM((n_plane, n_tgt * cap, enc_width), BF16),
            pltpu.VMEM((2 * half, enc_width), BF16),
            pltpu.VMEM((n_ids, n_plane * n_tgt * cap), BF16),
            pltpu.VMEM((n_ids, 2 * half), BF16),
            pltpu.VMEM((2 * half, n_ids), BF16),
            pltpu.VMEM((heads, 2 * half, 2 * HEAD_DIM), BF16),
            pltpu.VMEM((heads, n_ids, 2 * HEAD_DIM), BF16),
            pltpu.VMEM((n_ids, 2 * half), F32),
            pltpu.VMEM((heads, 2 * half, 2 * HEAD_DIM), BF16),
            pltpu.VMEM((heads, half, 2 * HEAD_DIM), BF16),
            pltpu.VMEM((2, heads, 32, 2 * HEAD_DIM), BF16),
            pltpu.VMEM((2, k_long, heads, 32, 2 * HEAD_DIM), BF16),
            pltpu.VMEM((n_ids, enc_width), BF16),
            pltpu.VMEM((n_plane, n_ids // n_plane, enc_width), BF16),
            pltpu.VMEM((n_ids, enc_width), BF16),
            dma, dma((n_tgt,)),
            dma((n_tgt,)), dma((n_tgt,)),
            dma, dma,
            dma, dma((2, nq, k_long)),
            dma, dma((nq,)),
            dma, dma((heads,)),
            dma, dma((2, nq, k_long)),
            dma, dma,
            dma, dma,
        ],
        compiler_params=pltpu.CompilerParams(
            collective_id=0, has_side_effects=True, vmem_limit_bytes=60 * 1024 * 1024
        ),
        name="layer",
    )(
        neighbour_ids.reshape(1, n_ids), embed_table, enc_gain.reshape(1, enc_width), weight,
        queries[0], grad_out[0],
    )
    attn, grad_query, weight_grad, grad_enc = out
    weight_grad = weight_grad[:, :e_rows].reshape(heads, e_rows, 2, HEAD_DIM).transpose(1, 2, 0, 3)
    return (
        attn[None],
        grad_query[None],
        weight_grad.reshape(1, e_rows, 2, local),
        grad_enc.reshape(spans, nbr, enc_width),
    )


def solution(mesh):
    in_specs = (
        P("dp", None),
        P(("dp", "mp"), None),
        P(),
        P("section", "dp", None, "mp"),
        P("section", "dp", "mp"),
        P("section", "dp", "mp"),
    )
    out_specs = (
        P("section", "dp", "mp"),
        P("section", "dp", "mp"),
        P("section", "dp", None, "mp"),
        P("dp", None, None),
    )
    sizes = (mesh.shape["dp"], mesh.shape["section"], mesh.shape["mp"])
    return jax.shard_map(
        functools.partial(body, *sizes), mesh=mesh, in_specs=in_specs, out_specs=out_specs,
        check_vma=False,
    )
```

```python
import functools
import math

import jax
import jax.numpy as jnp
from jax import lax
from jax.experimental import pallas as pl
from jax.experimental.pallas import tpu as pltpu
from jax.sharding import PartitionSpec as P

HEAD_DIM = 128
SPAN = 64
PACK = 16
HEAD_COLS = 2 * HEAD_DIM
MESH = pl.DeviceIdType.MESH
F32 = jnp.float32
BF16 = jnp.bfloat16
NT = (((1,), (1,)), ((), ()))
TN = (((0,), (0,)), ((), ()))


def dot(a, b, dims=(((1,), (0,)), ((), ()))):
    return lax.dot_general(a, b, dims, preferred_element_type=F32)


def iota(shape, axis):
    return lax.broadcasted_iota(jnp.int32, shape, axis)


def kernel(
    n_dp, n_sec, n_mp, cap, e_rows,
    ids_ref, table_ref, gain_ref, w_ref, q_ref, g_ref,
    attn_ref, gq_ref, wg_ref, genc_ref,
    ids_buf, pack_buf, land_buf, rows_buf, spread, pad_mat, place,
    enc_buf, enct_buf, wbuf, gbuf, pbuf, sib, sbuf, rbuf,
    esend, eland, gall,
    ids_send, ids_recv, pack_send, pack_recv, row_send, row_recv,
    ring_send, ring_recv, twin_send, twin_recv,
    half_send, half_recv, sum_send, sum_recv,
    part_send, part_recv, full_send, full_recv,
):
    nz = n_dp // 2
    n_plane = n_sec * n_mp
    n_tgt = n_dp // n_sec
    heads = wbuf.shape[1] // HEAD_COLS
    nq = 4 if heads % 4 == 0 else 1
    hq = heads // nq
    cq = hq * HEAD_COLS
    half = nz * 32
    spans, nbr = ids_ref.shape
    n_ids = spans * nbr
    owner_rows = table_ref.shape[0]
    out_rows = nbr // n_plane
    k_long = nz // 2
    k_short = nz - 1 - k_long
    group = 4 if heads % 4 == 0 else 1
    inv_root = 1.0 / math.sqrt(HEAD_DIM)

    me = lax.axis_index("dp")
    sec = lax.axis_index("section")
    mp = lax.axis_index("mp")
    z = me // 2
    core = lax.rem(me, 2)
    twin = 2 * z + (1 - core)
    here = sec * n_mp + mp
    asks = lax.rem(me, n_sec) == sec
    my_tgt = me // n_sec
    my_lane = lax.rem(me, n_sec)

    def up(step):
        return lax.rem(z + step + 2 * nz, nz)

    nexts = (2 * up(1) + core, 2 * up(-1) + core)

    def peer(j):
        p = lax.rem(here + j, n_plane)
        return (me, p // n_mp, lax.rem(p, n_mp))

    def remote(src, dst, send, recv, device):
        return pltpu.make_async_remote_copy(
            src_ref=src, dst_ref=dst, send_sem=send, recv_sem=recv,
            device_id=device, device_id_type=MESH,
        )

    def drain(ref, sem):
        pltpu.make_async_copy(ref, ref, sem).wait()

    barrier = pltpu.get_barrier_semaphore()

    def greet(device):
        pl.semaphore_signal(barrier, inc=1, device_id=device, device_id_type=MESH)

    greet((nexts[0], sec, mp))
    greet((nexts[1], sec, mp))
    greet((twin, sec, mp))

    @pl.loop(1, n_plane)
    def _(j):
        greet(peer(j))

    for k in range(n_tgt):
        other = sec + n_sec * k

        @pl.when(other != me)
        def _():
            greet((other, sec, mp))

        @pl.when(jnp.logical_or(other != me, my_lane != sec))
        def _():
            greet((other, my_lane, mp))

    expected = 3 + (n_plane - 1) + n_tgt
    expected = expected + jnp.where(asks, n_dp - 1 - 1, 0)
    pl.semaphore_wait(barrier, expected)

    def shard(src_z, parity, q):
        row = pl.multiple_of(parity * half + src_z * 32, 32)
        return wbuf.at[pl.ds(row, 32), pl.ds(q * cq, cq)]

    def ring_copy(q, way, k, src_z):
        block = shard(src_z, core, q)
        return remote(block, block, ring_send, ring_recv.at[way, q, k], (nexts[way], sec, mp))

    def twin_copy(q, src_z):
        block = shard(src_z, core, q)
        return remote(block, block, twin_send, twin_recv.at[q], (twin, sec, mp))

    def last_step(q, way):
        return k_long if (q + way) % 2 == 0 else k_short

    own = pl.multiple_of(core * half + z * 32, 32)
    wbuf[pl.ds(own, 32), :] = jnp.zeros((32, wbuf.shape[1]), BF16)
    for part in range(2):
        for h in range(heads):
            wbuf[pl.ds(own, e_rows), pl.ds(h * HEAD_COLS + part * HEAD_DIM, HEAD_DIM)] = w_ref[
                :, part, pl.ds(h * HEAD_DIM, HEAD_DIM)
            ]

    @pl.when(asks)
    def _():
        ids_buf[my_tgt] = ids_ref[...]

        @pl.loop(1, n_dp)
        def _(j):
            to = lax.rem(me + j, n_dp)
            remote(ids_ref, ids_buf.at[my_tgt], ids_send, ids_recv.at[my_tgt], (to, sec, mp)).start()

    for q in range(nq):
        for way in range(2):
            if last_step(q, way) > 0:
                ring_copy(q, way, 0, z).start()
        twin_copy(q, z).start()

    def gather_step(k, live, onward):
        for q in range(nq):
            for way in range(2):
                if not live(q, way):
                    continue
                src_z = up(-k) if way == 0 else up(k)
                ring_copy(q, way, k - 1, src_z).wait_recv()
                if onward(q, way):
                    ring_copy(q, way, k, src_z).start()
                twin_copy(q, src_z).start()

    def gather_steps(lo, hi):
        @pl.loop(lo, hi)
        def _(k):
            gather_step(k, lambda q, way: True, lambda q, way: True)

    def owner_of(ids):
        return ((ids.astype(F32) + 0.5) * (1.0 / owner_rows)).astype(jnp.int32)

    def base_of(ids):
        owner = owner_of(ids)
        dev = owner // n_mp
        slot = (lax.rem(dev, n_sec) * n_mp + lax.rem(owner, n_mp)) * (n_tgt * cap)
        return slot + (dev // n_sec) * cap

    ids = jnp.concatenate([ids_ref[c:c + 1, :] for c in range(spans)], axis=1)
    base_row = jnp.broadcast_to(base_of(ids).astype(F32), (n_ids, n_ids))
    row_no = iota((n_ids, n_ids), 0)
    col_no = iota((n_ids, n_ids), 1)
    base_col = jnp.sum(jnp.where(row_no == col_no, base_row, 0.0), axis=1, keepdims=True)
    same = jnp.logical_and(base_row == base_col, col_no < row_no)
    slot_col = jnp.sum(jnp.where(same, 1.0, 0.0), axis=1, keepdims=True)
    want = (base_col + slot_col).astype(jnp.int32)
    packed_rows = n_plane * n_tgt * cap
    place[...] = jnp.where(iota((n_ids, packed_rows), 1) == want, 1.0, 0.0).astype(BF16)

    wide = 2 * half
    enc_width = n_dp * e_rows
    pos = iota((wide, 1), 0)
    blk = pos // 32
    dev = 2 * lax.rem(blk, nz) + blk // nz
    inner = lax.rem(pos, 32)
    feature = jnp.where(inner < e_rows, dev * e_rows + inner, -1)
    pad_mat[...] = jnp.where(iota((wide, enc_width), 1) == feature, 1.0, 0.0).astype(BF16)

    first = max(1, min(2, k_short))
    second = max(first, min(4, k_short))
    gather_steps(1, first)

    for k in range(n_tgt):

        @pl.when(sec + n_sec * k != me)
        def _():
            drain(ids_buf.at[k], ids_recv.at[k])

    block_no = me * n_mp + mp
    upper = jnp.where(iota((n_ids, n_ids), 0) < iota((n_ids, n_ids), 1), 1.0, 0.0).astype(BF16)
    offs = jnp.concatenate(
        [
            jnp.concatenate(
                [jnp.broadcast_to(ids_buf[k, c:c + 1, :], (PACK, nbr)) for c in range(spans)], axis=1
            )
            for k in range(n_tgt)
        ],
        axis=0,
    ) - block_no * owner_rows
    mine = jnp.logical_and(offs >= 0, offs < owner_rows)
    slots = dot(jnp.where(mine, 1.0, 0.0).astype(BF16), upper)
    rank = lax.rem(iota((n_tgt * PACK, n_ids), 0), PACK).astype(F32)
    pick = jnp.logical_and(mine, slots == rank)
    wanted = jnp.sum(jnp.where(pick, offs.astype(F32) + 1.0, 0.0), axis=1, keepdims=True) - 1.0
    hot = jnp.where(
        iota((n_tgt * PACK, owner_rows), 1) == wanted.astype(jnp.int32), 1.0, 0.0
    ).astype(BF16)
    pack_buf[...] = dot(hot, table_ref[...]).astype(BF16).reshape(pack_buf.shape)

    for k in range(n_tgt):
        to = sec + n_sec * k
        away = jnp.logical_or(to != me, my_lane != sec)

        @pl.when(away)
        def _():
            remote(
                pack_buf.at[k], land_buf.at[my_tgt], pack_send.at[k], pack_recv.at[my_tgt],
                (to, my_lane, mp),
            ).start()

        @pl.when(jnp.logical_not(away))
        def _():
            land_buf[my_tgt] = pack_buf[k]

    gather_steps(first, second)

    for k in range(n_tgt):

        @pl.when(jnp.logical_or(sec + n_sec * k != me, my_lane != sec))
        def _():
            drain(land_buf.at[k], pack_recv.at[k])

    tight = n_tgt * cap
    row = iota((tight, n_tgt * PACK), 0)
    col = iota((tight, n_tgt * PACK), 1)
    squeeze = jnp.where((row // cap) * PACK + lax.rem(row, cap) == col, 1.0, 0.0).astype(BF16)
    landed = land_buf[...].reshape(n_tgt * PACK, enc_width)
    rows_buf[...] = dot(squeeze, landed).astype(BF16)
    spread[here] = rows_buf[...]

    @pl.loop(1, n_plane)
    def _(j):
        remote(rows_buf, spread.at[here], row_send, row_recv, peer(j)).start()

    gather_steps(second, k_short)
    if k_short >= 1:
        gather_step(k_short, lambda q, w: True, lambda q, w: last_step(q, w) > k_short)
    gather_step(k_long, lambda q, w: last_step(q, w) == k_long, lambda q, w: False)

    drain(spread.at[pl.ds(0, n_plane - 1)], row_recv)

    looked = dot(place[...], spread[...].reshape(packed_rows, enc_width))
    mean_square = jnp.mean(looked * looked, axis=-1, keepdims=True)
    encoded = (looked * lax.rsqrt(mean_square + 1e-06) * gain_ref[...][None, :]).astype(BF16)
    enc_buf[...] = dot(encoded, pad_mat[...], NT).astype(BF16)
    enct_buf[...] = dot(pad_mat[...], encoded, NT).astype(BF16)

    for q in range(nq):
        other_half = pl.ds(pl.multiple_of((1 - core) * half, 32), half)
        drain(wbuf.at[other_half, pl.ds(q * cq, cq)], twin_recv.at[q])

    def attend(c):
        tokens = pl.ds(c * SPAN, SPAN)
        rows = pl.ds(c * nbr, nbr)

        @pl.loop(0, heads // group)
        def _(i):
            start = pl.multiple_of(i * (group * HEAD_COLS), group * HEAD_COLS)
            weight = wbuf[:, pl.ds(start, group * HEAD_COLS)]
            keyval = dot(enc_buf[rows, :], weight).astype(BF16)
            lane = pl.multiple_of(i * (group * HEAD_DIM), group * HEAD_DIM)
            lanes = pl.ds(lane, group * HEAD_DIM)
            query = q_ref[tokens, lanes]
            grad = g_ref[tokens, lanes]

            def cols(array, width, hh, part=0, size=HEAD_DIM):
                return array[:, hh * width + part:hh * width + part + size]

            each = range(group)
            keys = [cols(keyval, HEAD_COLS, hh) for hh in each]
            values = [cols(keyval, HEAD_COLS, hh, HEAD_DIM) for hh in each]
            queries = [cols(query, HEAD_DIM, hh) for hh in each]
            grads = [cols(grad, HEAD_DIM, hh) for hh in each]
            scores = [dot(queries[hh], keys[hh], NT) * inv_root for hh in each]
            grad_probs = [dot(grads[hh], values[hh], NT) for hh in each]
            expos = [jnp.exp(x - jnp.max(x, axis=-1, keepdims=True)) for x in scores]
            probs = [x / jnp.sum(x, axis=-1, keepdims=True) for x in expos]
            probs_b = [x.astype(BF16) for x in probs]
            mixed = [jnp.sum(a * b, axis=-1, keepdims=True) for a, b in zip(grad_probs, probs)]
            grad_scores = [
                (p * (g - m) * inv_root).astype(BF16) for p, g, m in zip(probs, grad_probs, mixed)
            ]
            attn = [dot(probs_b[hh], values[hh]).astype(BF16) for hh in each]
            grad_q = [dot(grad_scores[hh], keys[hh]).astype(BF16) for hh in each]
            attn_ref[tokens, lanes] = jnp.concatenate(attn, axis=1)
            gq_ref[tokens, lanes] = jnp.concatenate(grad_q, axis=1)
            grad_kv = []
            for hh in each:
                grad_kv.append(dot(grad_scores[hh], queries[hh], TN).astype(BF16))
                grad_kv.append(dot(probs_b[hh], grads[hh], TN).astype(BF16))
            gbuf[rows, pl.ds(start, group * HEAD_COLS)] = jnp.concatenate(grad_kv, axis=1)

    def out_slice(c, p):
        return pl.ds(pl.multiple_of(c * nbr + p * out_rows, out_rows), out_rows)

    def send_parts(c):
        rows = pl.ds(c * nbr, nbr)
        term = dot(gbuf[rows, :], wbuf[...], NT).astype(BF16)
        esend[rows, :] = dot(term, pad_mat[...]).astype(BF16)
        eland[c, here] = esend[out_slice(c, here), :]

        @pl.loop(1, n_plane)
        def _(j):
            device = peer(j)
            p = device[1] * n_mp + device[2]
            remote(
                esend.at[out_slice(c, p), :], eland.at[c, here], part_send.at[c], part_recv.at[c],
                device,
            ).start()

    def send_sums(c):
        drain(eland.at[c, pl.ds(0, n_plane - 1)], part_recv.at[c])
        mine_rows = jnp.sum(eland[c].astype(F32), axis=0).astype(BF16)
        gall[out_slice(c, here), :] = mine_rows

        @pl.loop(1, n_plane)
        def _(j):
            block = gall.at[out_slice(c, here), :]
            remote(block, block, full_send.at[c], full_recv.at[c], peer(j)).start()

    def columns(q):
        return pl.ds(q * cq, cq)

    away_half = pl.ds(pl.multiple_of((1 - core) * half, 32), half)

    def weight_grad(q):
        pbuf[:, columns(q)] = dot(enct_buf[...], gbuf[:, columns(q)]).astype(BF16)
        remote(
            pbuf.at[away_half, columns(q)], sib.at[:, columns(q)], half_send, half_recv.at[q],
            (twin, sec, mp),
        ).start()

    def pair(q, dest_z):
        a = pbuf[pl.ds(pl.multiple_of(core * half + dest_z * 32, 32), 32), columns(q)]
        b = sib[pl.ds(pl.multiple_of(dest_z * 32, 32), 32), columns(q)]
        return a.astype(F32) + b.astype(F32)

    def sum_copy(src, q, way, k):
        return remote(
            src, rbuf.at[way, k, :, columns(q)], sum_send, sum_recv.at[way, q, k],
            (nexts[way], sec, mp),
        )

    def dest(way, steps):
        return up(steps) if way == 0 else up(-steps)

    def sum_first(q):
        drain(sib.at[:, columns(q)], half_recv.at[q])
        for way in range(2):
            steps = last_step(q, way)
            if steps > 0:
                block = sbuf.at[way, :, columns(q)]
                block[...] = pair(q, dest(way, steps)).astype(BF16)
                sum_copy(block, q, way, 0).start()

    def sum_step(k, live):
        for q in range(nq):
            for way in range(2):
                if not live(q, way):
                    continue
                block = rbuf.at[way, k - 1, :, columns(q)]
                sum_copy(block, q, way, k - 1).wait_recv()
                total = block[...].astype(F32) + pair(q, dest(way, last_step(q, way) - k))
                block[...] = total.astype(BF16)
                sum_copy(block, q, way, k).start()

    for c in range(spans):
        attend(c)
        if c < spans - 1:
            send_parts(c)
    lag = 2 if nq > 2 else 0
    for q in range(nq):
        weight_grad(q)
        if q == lag:
            send_parts(spans - 1)
        if q >= lag:
            sum_first(q - lag)
    for c in range(spans - 1):
        send_sums(c)
    for q in range(nq - lag, nq):
        sum_first(q)

    middle = max(1, min(4, k_short))

    @pl.loop(1, middle)
    def _(k):
        sum_step(k, lambda q, w: True)

    send_sums(spans - 1)

    @pl.loop(middle, k_short)
    def _(k):
        sum_step(k, lambda q, w: True)

    if k_short >= 1:
        sum_step(k_short, lambda q, w: last_step(q, w) > k_short)

    for q in range(nq):
        total = pair(q, z)
        for way in range(2):
            steps = last_step(q, way)
            if steps > 0:
                block = rbuf.at[way, steps - 1, :, columns(q)]
                sum_copy(block, q, way, steps - 1).wait_recv()
                total = total + block[...].astype(F32)
        total = total.astype(BF16)
        for hh in range(hq):
            for part in range(2):
                at = hh * HEAD_COLS + part * HEAD_DIM
                wg_ref[:, part, pl.ds((q * hq + hh) * HEAD_DIM, HEAD_DIM)] = total[
                    :e_rows, at:at + HEAD_DIM
                ]

    for c in range(spans):
        drain(gall.at[pl.ds(0, (n_plane - 1) * out_rows), :], full_recv.at[c])
    genc_ref[...] = gall[...]

    @pl.when(asks)
    def _():
        @pl.loop(1, n_dp)
        def _(j):
            drain(ids_ref, ids_send)

    for k in range(n_tgt):

        @pl.when(jnp.logical_or(sec + n_sec * k != me, my_lane != sec))
        def _():
            drain(pack_buf.at[k], pack_send.at[k])

    drain(spread.at[pl.ds(0, n_plane - 1)], row_send)
    sent = pl.ds(0, (nz - 1) * 32)
    drain(wbuf.at[sent, :], ring_send)
    drain(wbuf.at[pl.ds(0, half), :], twin_send)
    drain(sib, half_send)
    drain(sib.at[sent, :], sum_send)
    for c in range(spans):
        drain(eland.at[c, pl.ds(0, n_plane - 1)], part_send.at[c])
        drain(gall.at[pl.ds(0, (n_plane - 1) * out_rows), :], full_send.at[c])


def settle(*refs):
    count = len(refs) // 2
    sems = refs[-1]
    copies = [pltpu.make_async_copy(refs[i], refs[count + i], sems.at[i]) for i in range(count)]
    for copy in copies:
        copy.start()
    for copy in copies:
        copy.wait()


def body(n_dp, n_sec, n_mp, neighbour_ids, embed_table, enc_gain, kv_weight, queries, grad_out):
    spans, nbr = neighbour_ids.shape
    n_ids = spans * nbr
    owner_rows, enc_width = embed_table.shape
    e_rows, local = kv_weight.shape[1], kv_weight.shape[3]
    heads = local // HEAD_DIM
    tokens = queries.shape[1]
    cap = 3 * n_ids // (2 * n_dp * n_mp)
    nz, n_plane, n_tgt = n_dp // 2, n_sec * n_mp, n_dp // n_sec
    half = nz * 32
    nq = 4 if heads % 4 == 0 else 1
    k_long = nz // 2
    cols = heads * HEAD_COLS
    cols = heads * HEAD_COLS
    vmem = pl.BlockSpec(memory_space=pltpu.VMEM)
    dma = pltpu.SemaphoreType.DMA
    out = pl.pallas_call(
        functools.partial(kernel, n_dp, n_sec, n_mp, cap, e_rows),
        out_shape=(
            jax.ShapeDtypeStruct((tokens, local), BF16),
            jax.ShapeDtypeStruct((tokens, local), BF16),
            jax.ShapeDtypeStruct((e_rows, 2, local), BF16),
            jax.ShapeDtypeStruct((n_ids, enc_width), BF16),
        ),
        in_specs=[vmem] * 6,
        out_specs=(vmem,) * 4,
        scratch_shapes=[
            pltpu.VMEM((n_tgt, spans, nbr), jnp.int32),
            pltpu.VMEM((n_tgt, PACK, enc_width), BF16),
            pltpu.VMEM((n_tgt, PACK, enc_width), BF16),
            pltpu.VMEM((n_tgt * cap, enc_width), BF16),
            pltpu.VMEM((n_plane, n_tgt * cap, enc_width), BF16),
            pltpu.VMEM((2 * half, enc_width), BF16),
            pltpu.VMEM((n_ids, n_plane * n_tgt * cap), BF16),
            pltpu.VMEM((n_ids, 2 * half), BF16),
            pltpu.VMEM((2 * half, n_ids), BF16),
            pltpu.VMEM((2 * half, cols), BF16),
            pltpu.VMEM((n_ids, cols), BF16),
            pltpu.VMEM((2 * half, cols), BF16),
            pltpu.VMEM((half, cols), BF16),
            pltpu.VMEM((2, 32, cols), BF16),
            pltpu.VMEM((2, k_long, 32, cols), BF16),
            pltpu.VMEM((n_ids, enc_width), BF16),
            pltpu.VMEM((spans, n_plane, nbr // n_plane, enc_width), BF16),
            pltpu.VMEM((n_ids, enc_width), BF16),
            dma, dma((n_tgt,)),
            dma((n_tgt,)), dma((n_tgt,)),
            dma, dma,
            dma, dma((2, nq, k_long)),
            dma, dma((nq,)),
            dma, dma((nq,)),
            dma, dma((2, nq, k_long)),
            dma((spans,)), dma((spans,)),
            dma((spans,)), dma((spans,)),
        ],
        compiler_params=pltpu.CompilerParams(
            collective_id=0, has_side_effects=True, vmem_limit_bytes=60 * 1024 * 1024
        ),
        name="layer",
    )(
        neighbour_ids, embed_table, enc_gain, kv_weight[0],
        queries[0], grad_out[0],
    )
    hbm = pl.BlockSpec(memory_space=pl.ANY)
    attn, grad_query, weight_grad, grad_enc = pl.pallas_call(
        settle,
        out_shape=[jax.ShapeDtypeStruct(x.shape, x.dtype) for x in out],
        in_specs=[hbm] * len(out),
        out_specs=[hbm] * len(out),
        scratch_shapes=[dma((len(out),))],
        name="settle",
    )(*out)
    return (
        attn[None],
        grad_query[None],
        weight_grad[None],
        grad_enc.reshape(spans, nbr, enc_width),
    )


def solution(mesh):
    in_specs = (
        P("dp", None),
        P(("dp", "mp"), None),
        P(),
        P("section", "dp", None, "mp"),
        P("section", "dp", "mp"),
        P("section", "dp", "mp"),
    )
    out_specs = (
        P("section", "dp", "mp"),
        P("section", "dp", "mp"),
        P("section", "dp", None, "mp"),
        P("dp", None, None),
    )
    sizes = (mesh.shape["dp"], mesh.shape["section"], mesh.shape["mp"])
    return jax.shard_map(
        functools.partial(body, *sizes), mesh=mesh, in_specs=in_specs, out_specs=out_specs,
        check_vma=False,
    )
```

```python
import functools
import math

import jax
import jax.numpy as jnp
from jax import lax
from jax.experimental import pallas as pl
from jax.experimental.pallas import tpu as pltpu
from jax.sharding import PartitionSpec as P

HEAD_DIM = 128
SPAN = 64
PACK = 16
HEAD_COLS = 2 * HEAD_DIM
MESH = pl.DeviceIdType.MESH
F32 = jnp.float32
BF16 = jnp.bfloat16
NT = (((1,), (1,)), ((), ()))
TN = (((0,), (0,)), ((), ()))


def dot(a, b, dims=(((1,), (0,)), ((), ()))):
    return lax.dot_general(a, b, dims, preferred_element_type=F32)


def iota(shape, axis):
    return lax.broadcasted_iota(jnp.int32, shape, axis)


def kernel(
    n_dp, n_sec, n_mp, cap, e_rows,
    ids_ref, table_ref, gain_ref, w_ref, q_ref, g_ref,
    attn_ref, gq_ref, wg_ref, genc_ref,
    ids_buf, pack_buf, land_buf, spread, pad_mat, place,
    enc_buf, enct_buf, wbuf, gbuf, pbuf, sib, sbuf, rbuf, last_buf, last_out,
    esend, eland, gall,
    ids_send, ids_recv, pack_send, pack_recv, row_send, row_recv,
    ring_send, ring_recv, twin_send, twin_recv,
    half_send, half_recv, sum_send, sum_recv,
    part_send, part_recv, full_send, full_recv,
):
    nz = n_dp // 2
    n_plane = n_sec * n_mp
    n_tgt = n_dp // n_sec
    heads = wbuf.shape[1] // HEAD_COLS
    nq = 4 if heads % 4 == 0 else 1
    hq = heads // nq
    cq = hq * HEAD_COLS
    half = nz * 32
    spans, nbr = ids_ref.shape
    n_ids = spans * nbr
    owner_rows = table_ref.shape[0]
    out_rows = nbr // n_plane
    k_long = nz // 2
    k_short = nz - 1 - k_long
    group = 4 if heads % 4 == 0 else 1
    inv_root = 1.0 / math.sqrt(HEAD_DIM)

    me = lax.axis_index("dp")
    sec = lax.axis_index("section")
    mp = lax.axis_index("mp")
    z = me // 2
    core = lax.rem(me, 2)
    twin = 2 * z + (1 - core)
    here = sec * n_mp + mp
    ny, nx = spread.shape[:2]
    at_y = lax.rem(sec, ny)
    at_x = (sec // ny) * n_mp + mp
    asks = lax.rem(me, n_sec) == sec
    my_tgt = me // n_sec
    my_lane = lax.rem(me, n_sec)

    def up(step):
        return lax.rem(z + step + 2 * nz, nz)

    nexts = (2 * up(1) + core, 2 * up(-1) + core)

    def peer(j):
        p = lax.rem(here + j, n_plane)
        return (me, p // n_mp, lax.rem(p, n_mp))

    def peer_x(j):
        x = lax.rem(at_x + j, nx)
        return (me, (x // n_mp) * ny + at_y, lax.rem(x, n_mp))

    def peer_y(j):
        return (me, (at_x // n_mp) * ny + lax.rem(at_y + j, ny), mp)

    def remote(src, dst, send, recv, device):
        return pltpu.make_async_remote_copy(
            src_ref=src, dst_ref=dst, send_sem=send, recv_sem=recv,
            device_id=device, device_id_type=MESH,
        )

    def drain(ref, sem):
        pltpu.make_async_copy(ref, ref, sem).wait()

    own = pl.multiple_of(core * half + z * 32, 32)
    wbuf[pl.ds(own, 32), :] = jnp.zeros((32, wbuf.shape[1]), BF16)
    for part in range(2):
        for h in range(heads):
            wbuf[pl.ds(own, e_rows), pl.ds(h * HEAD_COLS + part * HEAD_DIM, HEAD_DIM)] = w_ref[
                :, part, pl.ds(h * HEAD_DIM, HEAD_DIM)
            ]

    def owner_of(ids):
        return ((ids.astype(F32) + 0.5) * (1.0 / owner_rows)).astype(jnp.int32)

    def base_of(ids):
        owner = owner_of(ids)
        dev = owner // n_mp
        dev_sec = lax.rem(dev, n_sec)
        slot = lax.rem(dev_sec, ny) * nx + (dev_sec // ny) * n_mp + lax.rem(owner, n_mp)
        return slot * (n_tgt * cap) + (dev // n_sec) * cap

    ids = jnp.concatenate([ids_ref[c:c + 1, :] for c in range(spans)], axis=1)
    base_row = jnp.broadcast_to(base_of(ids).astype(F32), (n_ids, n_ids))
    row_no = iota((n_ids, n_ids), 0)
    col_no = iota((n_ids, n_ids), 1)
    base_col = jnp.sum(jnp.where(row_no == col_no, base_row, 0.0), axis=1, keepdims=True)
    same = jnp.logical_and(base_row == base_col, col_no < row_no)
    slot_col = jnp.sum(jnp.where(same, 1.0, 0.0), axis=1, keepdims=True)
    want = (base_col + slot_col).astype(jnp.int32)
    packed_rows = n_plane * n_tgt * cap
    place[...] = jnp.where(iota((n_ids, packed_rows), 1) == want, 1.0, 0.0).astype(BF16)

    wide = 2 * half
    enc_width = n_dp * e_rows
    pos = iota((wide, 1), 0)
    blk = pos // 32
    dev = 2 * lax.rem(blk, nz) + blk // nz
    inner = lax.rem(pos, 32)
    feature = jnp.where(inner < e_rows, dev * e_rows + inner, -1)
    pad_mat[...] = jnp.where(iota((wide, enc_width), 1) == feature, 1.0, 0.0).astype(BF16)

    barrier = pltpu.get_barrier_semaphore()

    def greet(device):
        pl.semaphore_signal(barrier, inc=1, device_id=device, device_id_type=MESH)

    greet((nexts[0], sec, mp))
    greet((nexts[1], sec, mp))
    greet((twin, sec, mp))

    @pl.loop(1, n_plane)
    def _(j):
        greet(peer(j))

    for k in range(n_tgt):
        other = sec + n_sec * k

        @pl.when(other != me)
        def _():
            greet((other, sec, mp))

        @pl.when(jnp.logical_or(other != me, my_lane != sec))
        def _():
            greet((other, my_lane, mp))

    expected = 3 + (n_plane - 1) + n_tgt
    expected = expected + jnp.where(asks, n_dp - 1 - 1, 0)
    pl.semaphore_wait(barrier, expected)

    def shard(src_z, parity, q):
        row = pl.multiple_of(parity * half + src_z * 32, 32)
        return wbuf.at[pl.ds(row, 32), pl.ds(q * cq, cq)]

    def ring_copy(q, way, k, src_z):
        block = shard(src_z, core, q)
        return remote(block, block, ring_send, ring_recv.at[way, q, k], (nexts[way], sec, mp))

    def twin_copy(q, src_z):
        block = shard(src_z, core, q)
        return remote(block, block, twin_send, twin_recv.at[q], (twin, sec, mp))

    def last_step(q, way):
        return k_long if (q + way) % 2 == 0 else k_short

    @pl.when(asks)
    def _():
        ids_buf[my_tgt] = ids_ref[...]

        @pl.loop(1, n_dp)
        def _(j):
            to = lax.rem(me + j, n_dp)
            remote(ids_ref, ids_buf.at[my_tgt], ids_send, ids_recv.at[my_tgt], (to, sec, mp)).start()

    for q in range(nq):
        for way in range(2):
            if last_step(q, way) > 0:
                ring_copy(q, way, 0, z).start()
        twin_copy(q, z).start()

    def gather_step(k, live, onward):
        for q in range(nq):
            for way in range(2):
                if not live(q, way):
                    continue
                src_z = up(-k) if way == 0 else up(k)
                ring_copy(q, way, k - 1, src_z).wait_recv()
                if onward(q, way):
                    ring_copy(q, way, k, src_z).start()
                twin_copy(q, src_z).start()

    def gather_steps(lo, hi):
        @pl.loop(lo, hi)
        def _(k):
            gather_step(k, lambda q, way: True, lambda q, way: True)

    first = max(1, min(2, k_short))
    second = max(first, min(4, k_short))
    gather_steps(1, first)

    for k in range(n_tgt):

        @pl.when(sec + n_sec * k != me)
        def _():
            drain(ids_buf.at[k], ids_recv.at[k])

    block_no = me * n_mp + mp
    upper = jnp.where(iota((n_ids, n_ids), 0) < iota((n_ids, n_ids), 1), 1.0, 0.0).astype(BF16)
    offs = jnp.concatenate(
        [
            jnp.concatenate(
                [jnp.broadcast_to(ids_buf[k, c:c + 1, :], (PACK, nbr)) for c in range(spans)], axis=1
            )
            for k in range(n_tgt)
        ],
        axis=0,
    ) - block_no * owner_rows
    mine = jnp.logical_and(offs >= 0, offs < owner_rows)
    slots = dot(jnp.where(mine, 1.0, 0.0).astype(BF16), upper)
    rank = lax.rem(iota((n_tgt * PACK, n_ids), 0), PACK).astype(F32)
    pick = jnp.logical_and(mine, slots == rank)
    wanted = jnp.sum(jnp.where(pick, offs.astype(F32) + 1.0, 0.0), axis=1, keepdims=True) - 1.0
    hot = jnp.where(
        iota((n_tgt * PACK, owner_rows), 1) == wanted.astype(jnp.int32), 1.0, 0.0
    ).astype(BF16)
    pack_buf[...] = dot(hot, table_ref[...]).astype(BF16).reshape(pack_buf.shape)

    for k in range(n_tgt):
        to = sec + n_sec * k
        away = jnp.logical_or(to != me, my_lane != sec)

        @pl.when(away)
        def _():
            remote(
                pack_buf.at[k], land_buf.at[my_tgt], pack_send.at[k], pack_recv.at[my_tgt],
                (to, my_lane, mp),
            ).start()

        @pl.when(jnp.logical_not(away))
        def _():
            land_buf[my_tgt] = pack_buf[k]

    gather_steps(first, second)

    for k in range(n_tgt):

        @pl.when(jnp.logical_or(sec + n_sec * k != me, my_lane != sec))
        def _():
            drain(land_buf.at[k], pack_recv.at[k])

    tight = n_tgt * cap
    row = iota((tight, n_tgt * PACK), 0)
    col = iota((tight, n_tgt * PACK), 1)
    squeeze = jnp.where((row // cap) * PACK + lax.rem(row, cap) == col, 1.0, 0.0).astype(BF16)
    landed = land_buf[...].reshape(n_tgt * PACK, enc_width)
    spread[at_y, at_x] = dot(squeeze, landed).astype(BF16)

    cut = 128 * ((enc_width // 128 + 1) // 2)
    lanes_a, lanes_b = pl.ds(0, cut), pl.ds(cut, enc_width - cut)

    def spread_along(count, peer_of, block, stage):
        if count > 1:

            @pl.loop(1, count)
            def _(j):
                remote(block, block, row_send.at[stage], row_recv.at[stage], peer_of(j)).start()

    row_stages = (
        spread.at[0, pl.ds(0, nx - 1), :, lanes_a] if nx > 1 else None,
        spread.at[pl.ds(0, ny - 1), :, :, lanes_a] if ny > 1 else None,
        spread.at[pl.ds(0, ny - 1), 0, :, lanes_b] if ny > 1 else None,
        spread.at[:, pl.ds(0, nx - 1), :, lanes_b] if nx > 1 else None,
    )

    def row_drain(stage, sems):
        if row_stages[stage] is not None:
            drain(row_stages[stage], sems.at[stage])

    spread_along(nx, peer_x, spread.at[at_y, at_x, :, lanes_a], 0)
    spread_along(ny, peer_y, spread.at[at_y, at_x, :, lanes_b], 2)
    third = max(second, min(5, k_short))
    gather_steps(second, third)
    row_drain(0, row_recv)
    spread_along(ny, peer_y, spread.at[at_y, :, :, lanes_a], 1)
    row_drain(2, row_recv)
    spread_along(nx, peer_x, spread.at[:, at_x, :, lanes_b], 3)

    gather_steps(third, k_short)
    if k_short >= 1:
        gather_step(k_short, lambda q, w: True, lambda q, w: last_step(q, w) > k_short)
    gather_step(k_long, lambda q, w: last_step(q, w) == k_long, lambda q, w: False)

    row_drain(1, row_recv)
    row_drain(3, row_recv)

    looked = dot(place[...], spread[...].reshape(packed_rows, enc_width))
    mean_square = jnp.mean(looked * looked, axis=-1, keepdims=True)
    encoded = (looked * lax.rsqrt(mean_square + 1e-06) * gain_ref[...][None, :]).astype(BF16)
    enc_buf[...] = dot(encoded, pad_mat[...], NT).astype(BF16)
    enct_buf[...] = dot(pad_mat[...], encoded, NT).astype(BF16)

    for q in range(nq):
        other_half = pl.ds(pl.multiple_of((1 - core) * half, 32), half)
        drain(wbuf.at[other_half, pl.ds(q * cq, cq)], twin_recv.at[q])

    def attend(c, i):
        tokens = pl.ds(c * SPAN, SPAN)
        rows = pl.ds(c * nbr, nbr)
        start = i * (group * HEAD_COLS)
        weight = wbuf[:, pl.ds(start, group * HEAD_COLS)]
        keyval = dot(enc_buf[rows, :], weight).astype(BF16)
        lanes = pl.ds(i * (group * HEAD_DIM), group * HEAD_DIM)
        query = q_ref[tokens, lanes]
        grad = g_ref[tokens, lanes]

        def cols(array, width, hh, part=0, size=HEAD_DIM):
            return array[:, hh * width + part:hh * width + part + size]

        each = range(group)
        keys = [cols(keyval, HEAD_COLS, hh) for hh in each]
        values = [cols(keyval, HEAD_COLS, hh, HEAD_DIM) for hh in each]
        queries = [cols(query, HEAD_DIM, hh) for hh in each]
        grads = [cols(grad, HEAD_DIM, hh) for hh in each]
        scores = [dot(queries[hh], keys[hh], NT) * inv_root for hh in each]
        grad_probs = [dot(grads[hh], values[hh], NT) for hh in each]
        expos = [jnp.exp(x - jnp.max(x, axis=-1, keepdims=True)) for x in scores]
        probs = [x / jnp.sum(x, axis=-1, keepdims=True) for x in expos]
        probs_b = [x.astype(BF16) for x in probs]
        mixed = [jnp.sum(a * b, axis=-1, keepdims=True) for a, b in zip(grad_probs, probs)]
        grad_scores = [
            (p * (g - m) * inv_root).astype(BF16) for p, g, m in zip(probs, grad_probs, mixed)
        ]
        attn = [dot(probs_b[hh], values[hh]).astype(BF16) for hh in each]
        grad_q = [dot(grad_scores[hh], keys[hh]).astype(BF16) for hh in each]
        attn_ref[tokens, lanes] = jnp.concatenate(attn, axis=1)
        gq_ref[tokens, lanes] = jnp.concatenate(grad_q, axis=1)
        grad_kv = []
        for hh in each:
            grad_kv.append(dot(grad_scores[hh], queries[hh], TN).astype(BF16))
            grad_kv.append(dot(probs_b[hh], grads[hh], TN).astype(BF16))
        gbuf[rows, pl.ds(start, group * HEAD_COLS)] = jnp.concatenate(grad_kv, axis=1)

    def out_slice(c, p):
        return pl.ds(pl.multiple_of(c * nbr + p * out_rows, out_rows), out_rows)

    def send_parts(c):
        rows = pl.ds(c * nbr, nbr)
        term = dot(gbuf[rows, :], wbuf[...], NT).astype(BF16)
        esend[rows, :] = dot(term, pad_mat[...]).astype(BF16)
        eland[c, here] = esend[out_slice(c, here), :]

        @pl.loop(1, n_plane)
        def _(j):
            device = peer(j)
            p = device[1] * n_mp + device[2]
            remote(
                esend.at[out_slice(c, p), :], eland.at[c, here], part_send.at[c], part_recv.at[c],
                device,
            ).start()

    def send_sums(c):
        drain(eland.at[c, pl.ds(0, n_plane - 1)], part_recv.at[c])
        mine_rows = jnp.sum(eland[c].astype(F32), axis=0).astype(BF16)
        gall[out_slice(c, here), :] = mine_rows

        @pl.loop(1, n_plane)
        def _(j):
            block = gall.at[out_slice(c, here), :]
            remote(block, block, full_send.at[c], full_recv.at[c], peer(j)).start()

    def columns(q):
        return pl.ds(q * cq, cq)

    away_half = pl.ds(pl.multiple_of((1 - core) * half, 32), half)

    def weight_grad(q):
        pbuf[:, columns(q)] = dot(enct_buf[...], gbuf[:, columns(q)]).astype(BF16)
        remote(
            pbuf.at[away_half, columns(q)], sib.at[:, columns(q)], half_send, half_recv.at[q],
            (twin, sec, mp),
        ).start()

    def pair(q, dest_z):
        a = pbuf[pl.ds(pl.multiple_of(core * half + dest_z * 32, 32), 32), columns(q)]
        b = sib[pl.ds(pl.multiple_of(dest_z * 32, 32), 32), columns(q)]
        return a.astype(F32) + b.astype(F32)

    def narrow(q, way, k):
        return k < last_step(q, way) - 2

    def slot_of(q, way, k):
        if narrow(q, way, k):
            return rbuf.at[way, k, :, columns(q)]
        return last_buf.at[2 * way + k - last_step(q, way) + 2, :, columns(q)]

    def sum_copy(src, q, way, k):
        sem = sum_send.at[0 if narrow(q, way, k) else 1]
        return remote(
            src, slot_of(q, way, k), sem, sum_recv.at[way, q, k], (nexts[way], sec, mp)
        )

    def dest(way, steps):
        return up(steps) if way == 0 else up(-steps)

    def sum_first(q):
        drain(sib.at[:, columns(q)], half_recv.at[q])
        for way in range(2):
            steps = last_step(q, way)
            if steps > 0:
                block = (sbuf if narrow(q, way, 0) else last_out).at[way, :, columns(q)]
                block[...] = pair(q, dest(way, steps)).astype(block.dtype)
                sum_copy(block, q, way, 0).start()

    def sum_step(qs, k):
        for q in qs:
            for way in range(2):
                steps = last_step(q, way)
                if not 1 <= k < steps:
                    continue
                block = slot_of(q, way, k - 1)
                sum_copy(block, q, way, k - 1).wait_recv()
                total = block[...].astype(F32) + pair(q, dest(way, steps - k))
                if narrow(q, way, k - 1) and not narrow(q, way, k):
                    block = last_out.at[way, :, columns(q)]
                block[...] = total.astype(block.dtype)
                sum_copy(block, q, way, k).start()

    groups = heads // group
    per = nq // groups
    quarters = [range(i * per, (i + 1) * per) for i in range(groups)]

    for i in range(groups - 1):
        for c in range(spans):
            attend(c, i)
        for q in quarters[i]:
            weight_grad(q)
    ahead = 0
    for c in range(spans):
        attend(c, groups - 1)
        for i in range(groups - 1):
            if c == 0:
                for q in quarters[i]:
                    sum_first(q)
            else:
                sum_step(quarters[i], c)
                ahead = c
    for q in quarters[-1]:
        weight_grad(q)
    send_parts(0)
    ahead += 1
    for i in range(groups - 1):
        sum_step(quarters[i], ahead)
    for q in quarters[-1]:
        sum_first(q)
    for c in range(1, spans):
        send_parts(c)
    for k in range(1, k_long + 1):
        for i in range(groups - 1):
            sum_step(quarters[i], ahead + k)
        sum_step(quarters[-1], k)
        if k == min(4, k_long):
            for c in range(spans):
                send_sums(c)

    for q in range(nq):
        total = pair(q, z)
        for way in range(2):
            steps = last_step(q, way)
            if steps > 0:
                sum_copy(slot_of(q, way, steps - 1), q, way, steps - 1).wait_recv()
                total = total + slot_of(q, way, steps - 1)[...]
        total = total.astype(BF16)
        for hh in range(hq):
            for part in range(2):
                at = hh * HEAD_COLS + part * HEAD_DIM
                wg_ref[:, part, pl.ds((q * hq + hh) * HEAD_DIM, HEAD_DIM)] = total[
                    :e_rows, at:at + HEAD_DIM
                ]

    for c in range(spans):
        drain(gall.at[pl.ds(0, (n_plane - 1) * out_rows), :], full_recv.at[c])
    genc_ref[...] = gall[...]

    @pl.when(asks)
    def _():
        @pl.loop(1, n_dp)
        def _(j):
            drain(ids_ref, ids_send)

    for k in range(n_tgt):

        @pl.when(jnp.logical_or(sec + n_sec * k != me, my_lane != sec))
        def _():
            drain(pack_buf.at[k], pack_send.at[k])

    for stage in range(4):
        row_drain(stage, row_send)
    sent = pl.ds(0, (nz - 1) * 32)
    drain(wbuf.at[sent, :], ring_send)
    drain(wbuf.at[pl.ds(0, half), :], twin_send)
    drain(sib, half_send)
    if k_long > 2:
        narrow_sent = pl.ds(0, (k_long - 2 + max(0, k_short - 2)) * 32)
        drain(sib.at[narrow_sent, :], sum_send.at[0])
    last_two = min(2, k_long) + min(2, k_short)
    drain(last_buf.at[pl.ds(0, last_two)], sum_send.at[1])
    for c in range(spans):
        drain(eland.at[c, pl.ds(0, n_plane - 1)], part_send.at[c])
        drain(gall.at[pl.ds(0, (n_plane - 1) * out_rows), :], full_send.at[c])


def settle(*refs):
    count = len(refs) // 2
    sems = refs[-1]
    copies = [pltpu.make_async_copy(refs[i], refs[count + i], sems.at[i]) for i in range(count)]
    for copy in copies:
        copy.start()
    for copy in copies:
        copy.wait()


def body(n_dp, n_sec, n_mp, neighbour_ids, embed_table, enc_gain, kv_weight, queries, grad_out):
    spans, nbr = neighbour_ids.shape
    n_ids = spans * nbr
    owner_rows, enc_width = embed_table.shape
    e_rows, local = kv_weight.shape[1], kv_weight.shape[3]
    heads = local // HEAD_DIM
    tokens = queries.shape[1]
    cap = 3 * n_ids // (2 * n_dp * n_mp)
    nz, n_plane, n_tgt = n_dp // 2, n_sec * n_mp, n_dp // n_sec
    ny = max(1, n_sec // 2)
    half = nz * 32
    nq = 4 if heads % 4 == 0 else 1
    k_long = nz // 2
    cols = heads * HEAD_COLS
    cols = heads * HEAD_COLS
    vmem = pl.BlockSpec(memory_space=pltpu.VMEM)
    dma = pltpu.SemaphoreType.DMA
    out = pl.pallas_call(
        functools.partial(kernel, n_dp, n_sec, n_mp, cap, e_rows),
        out_shape=(
            jax.ShapeDtypeStruct((tokens, local), BF16),
            jax.ShapeDtypeStruct((tokens, local), BF16),
            jax.ShapeDtypeStruct((e_rows, 2, local), BF16),
            jax.ShapeDtypeStruct((n_ids, enc_width), BF16),
        ),
        in_specs=[vmem] * 6,
        out_specs=(vmem,) * 4,
        scratch_shapes=[
            pltpu.VMEM((n_tgt, spans, nbr), jnp.int32),
            pltpu.VMEM((n_tgt, PACK, enc_width), BF16),
            pltpu.VMEM((n_tgt, PACK, enc_width), BF16),
            pltpu.VMEM((ny, n_plane // ny, n_tgt * cap, enc_width), BF16),
            pltpu.VMEM((2 * half, enc_width), BF16),
            pltpu.VMEM((n_ids, n_plane * n_tgt * cap), BF16),
            pltpu.VMEM((n_ids, 2 * half), BF16),
            pltpu.VMEM((2 * half, n_ids), BF16),
            pltpu.VMEM((2 * half, cols), BF16),
            pltpu.VMEM((n_ids, cols), BF16),
            pltpu.VMEM((2 * half, cols), BF16),
            pltpu.VMEM((half, cols), BF16),
            pltpu.VMEM((2, 32, cols), BF16),
            pltpu.VMEM((2, k_long, 32, cols), BF16),
            pltpu.VMEM((4, 32, cols), F32),
            pltpu.VMEM((2, 32, cols), F32),
            pltpu.VMEM((n_ids, enc_width), BF16),
            pltpu.VMEM((spans, n_plane, nbr // n_plane, enc_width), BF16),
            pltpu.VMEM((n_ids, enc_width), BF16),
            dma, dma((n_tgt,)),
            dma((n_tgt,)), dma((n_tgt,)),
            dma((4,)), dma((4,)),
            dma, dma((2, nq, k_long)),
            dma, dma((nq,)),
            dma, dma((nq,)),
            dma((2,)), dma((2, nq, k_long)),
            dma((spans,)), dma((spans,)),
            dma((spans,)), dma((spans,)),
        ],
        compiler_params=pltpu.CompilerParams(
            collective_id=0, has_side_effects=True, vmem_limit_bytes=60 * 1024 * 1024
        ),
        name="layer",
    )(
        neighbour_ids, embed_table, enc_gain, kv_weight[0],
        queries[0], grad_out[0],
    )
    hbm = pl.BlockSpec(memory_space=pl.ANY)
    attn, grad_query, weight_grad, grad_enc = pl.pallas_call(
        settle,
        out_shape=[jax.ShapeDtypeStruct(x.shape, x.dtype) for x in out],
        in_specs=[vmem] * len(out),
        out_specs=[hbm] * len(out),
        scratch_shapes=[dma((len(out),))],
        name="settle",
    )(*out)
    return (
        attn[None],
        grad_query[None],
        weight_grad[None],
        grad_enc.reshape(spans, nbr, enc_width),
    )


def solution(mesh):
    in_specs = (
        P("dp", None),
        P(("dp", "mp"), None),
        P(),
        P("section", "dp", None, "mp"),
        P("section", "dp", "mp"),
        P("section", "dp", "mp"),
    )
    out_specs = (
        P("section", "dp", "mp"),
        P("section", "dp", "mp"),
        P("section", "dp", None, "mp"),
        P("dp", None, None),
    )
    sizes = (mesh.shape["dp"], mesh.shape["section"], mesh.shape["mp"])
    return jax.shard_map(
        functools.partial(body, *sizes), mesh=mesh, in_specs=in_specs, out_specs=out_specs,
        check_vma=False,
    )
```

```python
import functools
import math

import jax
import jax.numpy as jnp
from jax import lax
from jax.experimental import pallas as pl
from jax.experimental.pallas import tpu as pltpu
from jax.sharding import PartitionSpec as P

HEAD_DIM = 128
SPAN = 64
PACK = 16
HEAD_COLS = 2 * HEAD_DIM
MESH = pl.DeviceIdType.MESH
F32 = jnp.float32
BF16 = jnp.bfloat16
NT = (((1,), (1,)), ((), ()))
TN = (((0,), (0,)), ((), ()))


def dot(a, b, dims=(((1,), (0,)), ((), ()))):
    return lax.dot_general(a, b, dims, preferred_element_type=F32)


def iota(shape, axis):
    return lax.broadcasted_iota(jnp.int32, shape, axis)


def kernel(
    n_dp, n_sec, n_mp, cap, e_rows,
    ids_ref, table_ref, gain_ref, w_ref, q_ref, g_ref,
    attn_ref, gq_ref, wg_ref, genc_ref,
    ids_buf, pack_buf, land_buf, spread, pad_mat, place,
    enc_buf, enct_buf, wbuf, gbuf, pbuf, sib, sbuf, rbuf, last_buf, last_out,
    esend, eland, gall,
    ids_send, ids_recv, pack_send, pack_recv, row_send, row_recv,
    ring_send, ring_recv, twin_send, twin_recv,
    half_send, half_recv, sum_send, sum_recv,
    part_send, part_recv, full_send, full_recv,
):
    nz = n_dp // 2
    n_plane = n_sec * n_mp
    n_tgt = n_dp // n_sec
    heads = wbuf.shape[1] // HEAD_COLS
    nq = 4 if heads % 4 == 0 else 1
    hq = heads // nq
    cq = hq * HEAD_COLS
    half = nz * 32
    spans, nbr = ids_ref.shape
    n_ids = spans * nbr
    owner_rows = table_ref.shape[0]
    out_rows = nbr // n_plane
    k_long = nz // 2
    k_short = nz - 1 - k_long
    group = 4 if heads % 4 == 0 else 1
    inv_root = 1.0 / math.sqrt(HEAD_DIM)

    me = lax.axis_index("dp")
    sec = lax.axis_index("section")
    mp = lax.axis_index("mp")
    z = me // 2
    core = lax.rem(me, 2)
    twin = 2 * z + (1 - core)
    here = sec * n_mp + mp
    ny, nx = spread.shape[:2]
    at_y = lax.rem(sec, ny)
    at_x = (sec // ny) * n_mp + mp
    asks = lax.rem(me, n_sec) == sec
    my_tgt = me // n_sec
    my_lane = lax.rem(me, n_sec)

    def up(step):
        return lax.rem(z + step + 2 * nz, nz)

    nexts = (2 * up(1) + core, 2 * up(-1) + core)

    def peer(j):
        p = lax.rem(here + j, n_plane)
        return (me, p // n_mp, lax.rem(p, n_mp))

    def peer_x(j):
        x = lax.rem(at_x + j, nx)
        return (me, (x // n_mp) * ny + at_y, lax.rem(x, n_mp))

    def peer_y(j):
        return (me, (at_x // n_mp) * ny + lax.rem(at_y + j, ny), mp)

    def remote(src, dst, send, recv, device):
        return pltpu.make_async_remote_copy(
            src_ref=src, dst_ref=dst, send_sem=send, recv_sem=recv,
            device_id=device, device_id_type=MESH,
        )

    def drain(ref, sem):
        pltpu.make_async_copy(ref, ref, sem).wait()

    own = pl.multiple_of(core * half + z * 32, 32)
    wbuf[pl.ds(own, 32), :] = jnp.zeros((32, wbuf.shape[1]), BF16)
    for part in range(2):
        for h in range(heads):
            wbuf[pl.ds(own, e_rows), pl.ds(h * HEAD_COLS + part * HEAD_DIM, HEAD_DIM)] = w_ref[
                :, part, pl.ds(h * HEAD_DIM, HEAD_DIM)
            ]

    def owner_of(ids):
        return ((ids.astype(F32) + 0.5) * (1.0 / owner_rows)).astype(jnp.int32)

    def base_of(ids):
        owner = owner_of(ids)
        dev = owner // n_mp
        dev_sec = lax.rem(dev, n_sec)
        slot = lax.rem(dev_sec, ny) * nx + (dev_sec // ny) * n_mp + lax.rem(owner, n_mp)
        return slot * (n_tgt * cap) + (dev // n_sec) * cap

    ids = jnp.concatenate([ids_ref[c:c + 1, :] for c in range(spans)], axis=1)
    base_row = jnp.broadcast_to(base_of(ids).astype(F32), (n_ids, n_ids))
    row_no = iota((n_ids, n_ids), 0)
    col_no = iota((n_ids, n_ids), 1)
    base_col = jnp.sum(jnp.where(row_no == col_no, base_row, 0.0), axis=1, keepdims=True)
    same = jnp.logical_and(base_row == base_col, col_no < row_no)
    slot_col = jnp.sum(jnp.where(same, 1.0, 0.0), axis=1, keepdims=True)
    want = (base_col + slot_col).astype(jnp.int32)
    packed_rows = n_plane * n_tgt * cap
    place[...] = jnp.where(iota((n_ids, packed_rows), 1) == want, 1.0, 0.0).astype(BF16)

    wide = 2 * half
    enc_width = n_dp * e_rows
    pos = iota((wide, 1), 0)
    blk = pos // 32
    dev = 2 * lax.rem(blk, nz) + blk // nz
    inner = lax.rem(pos, 32)
    feature = jnp.where(inner < e_rows, dev * e_rows + inner, -1)
    pad_mat[...] = jnp.where(iota((wide, enc_width), 1) == feature, 1.0, 0.0).astype(BF16)

    barrier = pltpu.get_barrier_semaphore()

    def greet(device):
        pl.semaphore_signal(barrier, inc=1, device_id=device, device_id_type=MESH)

    greet((nexts[0], sec, mp))
    greet((nexts[1], sec, mp))
    greet((twin, sec, mp))

    @pl.loop(1, nx)
    def _(j):
        greet(peer_x(j))

    @pl.loop(1, ny)
    def _(j):
        greet(peer_y(j))

    for k in range(n_tgt):
        other = sec + n_sec * k

        @pl.when(other != me)
        def _():
            greet((other, sec, mp))

        @pl.when(jnp.logical_or(other != me, my_lane != sec))
        def _():
            greet((other, my_lane, mp))

    expected = 3 + (nx - 1) + (ny - 1) + n_tgt
    expected = expected + jnp.where(asks, n_dp - 1 - 1, 0)
    pl.semaphore_wait(barrier, expected)

    def shard(src_z, parity, q):
        row = pl.multiple_of(parity * half + src_z * 32, 32)
        return wbuf.at[pl.ds(row, 32), pl.ds(q * cq, cq)]

    def ring_copy(q, way, k, src_z):
        block = shard(src_z, core, q)
        return remote(block, block, ring_send, ring_recv.at[way, q, k], (nexts[way], sec, mp))

    def twin_copy(q, src_z):
        block = shard(src_z, core, q)
        return remote(block, block, twin_send, twin_recv.at[q], (twin, sec, mp))

    def last_step(q, way):
        return k_long if (q + way) % 2 == 0 else k_short

    @pl.when(asks)
    def _():
        ids_buf[my_tgt] = ids_ref[...]

        @pl.loop(1, n_dp)
        def _(j):
            to = lax.rem(me + j, n_dp)
            remote(ids_ref, ids_buf.at[my_tgt], ids_send, ids_recv.at[my_tgt], (to, sec, mp)).start()

    for q in range(nq):
        for way in range(2):
            if last_step(q, way) > 0:
                ring_copy(q, way, 0, z).start()
        twin_copy(q, z).start()

    def gather_step(k, live, onward):
        for q in range(nq):
            for way in range(2):
                if not live(q, way):
                    continue
                src_z = up(-k) if way == 0 else up(k)
                ring_copy(q, way, k - 1, src_z).wait_recv()
                if onward(q, way):
                    ring_copy(q, way, k, src_z).start()
                twin_copy(q, src_z).start()

    def gather_steps(lo, hi):
        @pl.loop(lo, hi)
        def _(k):
            gather_step(k, lambda q, way: True, lambda q, way: True)

    first = max(1, min(2, k_short))
    second = max(first, min(4, k_short))
    gather_steps(1, first)

    for k in range(n_tgt):

        @pl.when(sec + n_sec * k != me)
        def _():
            drain(ids_buf.at[k], ids_recv.at[k])

    block_no = me * n_mp + mp
    upper = jnp.where(iota((n_ids, n_ids), 0) < iota((n_ids, n_ids), 1), 1.0, 0.0).astype(BF16)
    offs = jnp.concatenate(
        [
            jnp.concatenate(
                [jnp.broadcast_to(ids_buf[k, c:c + 1, :], (PACK, nbr)) for c in range(spans)], axis=1
            )
            for k in range(n_tgt)
        ],
        axis=0,
    ) - block_no * owner_rows
    mine = jnp.logical_and(offs >= 0, offs < owner_rows)
    slots = dot(jnp.where(mine, 1.0, 0.0).astype(BF16), upper)
    rank = lax.rem(iota((n_tgt * PACK, n_ids), 0), PACK).astype(F32)
    pick = jnp.logical_and(mine, slots == rank)
    wanted = jnp.sum(jnp.where(pick, offs.astype(F32) + 1.0, 0.0), axis=1, keepdims=True) - 1.0
    hot = jnp.where(
        iota((n_tgt * PACK, owner_rows), 1) == wanted.astype(jnp.int32), 1.0, 0.0
    ).astype(BF16)
    pack_buf[...] = dot(hot, table_ref[...]).astype(BF16).reshape(pack_buf.shape)

    for k in range(n_tgt):
        to = sec + n_sec * k
        away = jnp.logical_or(to != me, my_lane != sec)

        @pl.when(away)
        def _():
            remote(
                pack_buf.at[k], land_buf.at[my_tgt], pack_send.at[k], pack_recv.at[my_tgt],
                (to, my_lane, mp),
            ).start()

        @pl.when(jnp.logical_not(away))
        def _():
            land_buf[my_tgt] = pack_buf[k]

    gather_steps(first, second)

    for k in range(n_tgt):

        @pl.when(jnp.logical_or(sec + n_sec * k != me, my_lane != sec))
        def _():
            drain(land_buf.at[k], pack_recv.at[k])

    tight = n_tgt * cap
    row = iota((tight, n_tgt * PACK), 0)
    col = iota((tight, n_tgt * PACK), 1)
    squeeze = jnp.where((row // cap) * PACK + lax.rem(row, cap) == col, 1.0, 0.0).astype(BF16)
    landed = land_buf[...].reshape(n_tgt * PACK, enc_width)
    spread[at_y, at_x] = dot(squeeze, landed).astype(BF16)

    cut = 128 * ((enc_width // 128 + 1) // 2)
    lanes_a, lanes_b = pl.ds(0, cut), pl.ds(cut, enc_width - cut)

    def spread_along(count, peer_of, block, stage):
        if count > 1:

            @pl.loop(1, count)
            def _(j):
                remote(block, block, row_send.at[stage], row_recv.at[stage], peer_of(j)).start()

    row_stages = (
        spread.at[0, pl.ds(0, nx - 1), :, lanes_a] if nx > 1 else None,
        spread.at[pl.ds(0, ny - 1), :, :, lanes_a] if ny > 1 else None,
        spread.at[pl.ds(0, ny - 1), 0, :, lanes_b] if ny > 1 else None,
        spread.at[:, pl.ds(0, nx - 1), :, lanes_b] if nx > 1 else None,
    )

    def row_drain(stage, sems):
        if row_stages[stage] is not None:
            drain(row_stages[stage], sems.at[stage])

    spread_along(nx, peer_x, spread.at[at_y, at_x, :, lanes_a], 0)
    spread_along(ny, peer_y, spread.at[at_y, at_x, :, lanes_b], 2)
    third = max(second, min(5, k_short))
    gather_steps(second, third)
    row_drain(0, row_recv)
    spread_along(ny, peer_y, spread.at[at_y, :, :, lanes_a], 1)
    row_drain(2, row_recv)
    spread_along(nx, peer_x, spread.at[:, at_x, :, lanes_b], 3)

    gather_steps(third, k_short)
    if k_short >= 1:
        gather_step(k_short, lambda q, w: True, lambda q, w: last_step(q, w) > k_short)
    gather_step(k_long, lambda q, w: last_step(q, w) == k_long, lambda q, w: False)

    row_drain(1, row_recv)
    row_drain(3, row_recv)

    looked = dot(place[...], spread[...].reshape(packed_rows, enc_width))
    mean_square = jnp.mean(looked * looked, axis=-1, keepdims=True)
    encoded = (looked * lax.rsqrt(mean_square + 1e-06) * gain_ref[...][None, :]).astype(BF16)
    enc_buf[...] = dot(encoded, pad_mat[...], NT).astype(BF16)
    enct_buf[...] = dot(pad_mat[...], encoded, NT).astype(BF16)

    for q in range(nq):
        other_half = pl.ds(pl.multiple_of((1 - core) * half, 32), half)
        drain(wbuf.at[other_half, pl.ds(q * cq, cq)], twin_recv.at[q])

    def attend(c, i):
        tokens = pl.ds(c * SPAN, SPAN)
        rows = pl.ds(c * nbr, nbr)
        start = i * (group * HEAD_COLS)
        weight = wbuf[:, pl.ds(start, group * HEAD_COLS)]
        keyval = dot(enc_buf[rows, :], weight).astype(BF16)
        lanes = pl.ds(i * (group * HEAD_DIM), group * HEAD_DIM)
        query = q_ref[tokens, lanes]
        grad = g_ref[tokens, lanes]

        def cols(array, width, hh, part=0, size=HEAD_DIM):
            return array[:, hh * width + part:hh * width + part + size]

        each = range(group)
        keys = [cols(keyval, HEAD_COLS, hh) for hh in each]
        values = [cols(keyval, HEAD_COLS, hh, HEAD_DIM) for hh in each]
        queries = [cols(query, HEAD_DIM, hh) for hh in each]
        grads = [cols(grad, HEAD_DIM, hh) for hh in each]
        scores = [dot(queries[hh], keys[hh], NT) * inv_root for hh in each]
        grad_probs = [dot(grads[hh], values[hh], NT) for hh in each]
        expos = [jnp.exp(x - jnp.max(x, axis=-1, keepdims=True)) for x in scores]
        probs = [x / jnp.sum(x, axis=-1, keepdims=True) for x in expos]
        probs_b = [x.astype(BF16) for x in probs]
        mixed = [jnp.sum(a * b, axis=-1, keepdims=True) for a, b in zip(grad_probs, probs)]
        grad_scores = [
            (p * (g - m) * inv_root).astype(BF16) for p, g, m in zip(probs, grad_probs, mixed)
        ]
        attn = [dot(probs_b[hh], values[hh]).astype(BF16) for hh in each]
        grad_q = [dot(grad_scores[hh], keys[hh]).astype(BF16) for hh in each]
        attn_ref[tokens, lanes] = jnp.concatenate(attn, axis=1)
        gq_ref[tokens, lanes] = jnp.concatenate(grad_q, axis=1)
        grad_kv = []
        for hh in each:
            grad_kv.append(dot(grad_scores[hh], queries[hh], TN).astype(BF16))
            grad_kv.append(dot(probs_b[hh], grads[hh], TN).astype(BF16))
        gbuf[rows, pl.ds(start, group * HEAD_COLS)] = jnp.concatenate(grad_kv, axis=1)

    def out_slice(c, p):
        return pl.ds(pl.multiple_of(c * nbr + p * out_rows, out_rows), out_rows)

    def send_parts(c):
        rows = pl.ds(c * nbr, nbr)
        term = dot(gbuf[rows, :], wbuf[...], NT).astype(BF16)
        esend[rows, :] = dot(term, pad_mat[...]).astype(BF16)
        eland[c, here] = esend[out_slice(c, here), :]

        @pl.loop(1, n_plane)
        def _(j):
            device = peer(j)
            p = device[1] * n_mp + device[2]
            remote(
                esend.at[out_slice(c, p), :], eland.at[c, here], part_send.at[c], part_recv.at[c],
                device,
            ).start()

    def send_sums(c):
        drain(eland.at[c, pl.ds(0, n_plane - 1)], part_recv.at[c])
        mine_rows = jnp.sum(eland[c].astype(F32), axis=0).astype(BF16)
        gall[out_slice(c, here), :] = mine_rows

        @pl.loop(1, n_plane)
        def _(j):
            block = gall.at[out_slice(c, here), :]
            remote(block, block, full_send.at[c], full_recv.at[c], peer(j)).start()

    def columns(q):
        return pl.ds(q * cq, cq)

    away_half = pl.ds(pl.multiple_of((1 - core) * half, 32), half)

    def weight_grad(q):
        pbuf[:, columns(q)] = dot(enct_buf[...], gbuf[:, columns(q)]).astype(BF16)
        remote(
            pbuf.at[away_half, columns(q)], sib.at[:, columns(q)], half_send, half_recv.at[q],
            (twin, sec, mp),
        ).start()

    def pair(q, dest_z):
        a = pbuf[pl.ds(pl.multiple_of(core * half + dest_z * 32, 32), 32), columns(q)]
        b = sib[pl.ds(pl.multiple_of(dest_z * 32, 32), 32), columns(q)]
        return a.astype(F32) + b.astype(F32)

    def narrow(q, way, k):
        return k < last_step(q, way) - 2

    def slot_of(q, way, k):
        if narrow(q, way, k):
            return rbuf.at[way, k, :, columns(q)]
        return last_buf.at[2 * way + k - last_step(q, way) + 2, :, columns(q)]

    def sum_copy(src, q, way, k):
        sem = sum_send.at[0 if narrow(q, way, k) else 1]
        return remote(
            src, slot_of(q, way, k), sem, sum_recv.at[way, q, k], (nexts[way], sec, mp)
        )

    def dest(way, steps):
        return up(steps) if way == 0 else up(-steps)

    def sum_first(q):
        drain(sib.at[:, columns(q)], half_recv.at[q])
        for way in range(2):
            steps = last_step(q, way)
            if steps > 0:
                block = (sbuf if narrow(q, way, 0) else last_out).at[way, :, columns(q)]
                block[...] = pair(q, dest(way, steps)).astype(block.dtype)
                sum_copy(block, q, way, 0).start()

    def sum_step(qs, k):
        for q in qs:
            for way in range(2):
                steps = last_step(q, way)
                if not 1 <= k < steps:
                    continue
                block = slot_of(q, way, k - 1)
                sum_copy(block, q, way, k - 1).wait_recv()
                total = block[...].astype(F32) + pair(q, dest(way, steps - k))
                if narrow(q, way, k - 1) and not narrow(q, way, k):
                    block = last_out.at[way, :, columns(q)]
                block[...] = total.astype(block.dtype)
                sum_copy(block, q, way, k).start()

    groups = heads // group
    per = nq // groups
    quarters = [range(i * per, (i + 1) * per) for i in range(groups)]

    for i in range(groups - 1):
        for c in range(spans):
            attend(c, i)
        for q in quarters[i]:
            weight_grad(q)
    ahead = 0
    for c in range(spans):
        attend(c, groups - 1)
        for i in range(groups - 1):
            if c == 0:
                for q in quarters[i]:
                    sum_first(q)
            else:
                sum_step(quarters[i], c)
                ahead = c
    for q in quarters[-1]:
        weight_grad(q)
    ahead += 1
    for i in range(groups - 1):
        sum_step(quarters[i], ahead)
    for q in quarters[-1]:
        sum_first(q)
    for c in range(spans):
        send_parts(c)
    for k in range(1, k_long + 1):
        for i in range(groups - 1):
            sum_step(quarters[i], ahead + k)
        sum_step(quarters[-1], k)
        if k == min(4, k_long):
            for c in range(spans):
                send_sums(c)

    for q in range(nq):
        total = pair(q, z)
        for way in range(2):
            steps = last_step(q, way)
            if steps > 0:
                sum_copy(slot_of(q, way, steps - 1), q, way, steps - 1).wait_recv()
                total = total + slot_of(q, way, steps - 1)[...]
        total = total.astype(BF16)
        for hh in range(hq):
            for part in range(2):
                at = hh * HEAD_COLS + part * HEAD_DIM
                wg_ref[:, part, pl.ds((q * hq + hh) * HEAD_DIM, HEAD_DIM)] = total[
                    :e_rows, at:at + HEAD_DIM
                ]

    for c in range(spans):
        drain(gall.at[pl.ds(0, (n_plane - 1) * out_rows), :], full_recv.at[c])
    genc_ref[...] = gall[...]

    @pl.when(asks)
    def _():
        @pl.loop(1, n_dp)
        def _(j):
            drain(ids_ref, ids_send)

    for k in range(n_tgt):

        @pl.when(jnp.logical_or(sec + n_sec * k != me, my_lane != sec))
        def _():
            drain(pack_buf.at[k], pack_send.at[k])

    for stage in range(4):
        row_drain(stage, row_send)
    sent = pl.ds(0, (nz - 1) * 32)
    drain(wbuf.at[sent, :], ring_send)
    drain(wbuf.at[pl.ds(0, half), :], twin_send)
    drain(sib, half_send)
    if k_long > 2:
        narrow_sent = pl.ds(0, (k_long - 2 + max(0, k_short - 2)) * 32)
        drain(sib.at[narrow_sent, :], sum_send.at[0])
    last_two = min(2, k_long) + min(2, k_short)
    drain(last_buf.at[pl.ds(0, last_two)], sum_send.at[1])
    for c in range(spans):
        drain(eland.at[c, pl.ds(0, n_plane - 1)], part_send.at[c])
        drain(gall.at[pl.ds(0, (n_plane - 1) * out_rows), :], full_send.at[c])


def settle(*refs):
    count = len(refs) // 2
    sems = refs[-1]
    copies = [pltpu.make_async_copy(refs[i], refs[count + i], sems.at[i]) for i in range(count)]
    for copy in copies:
        copy.start()
    for copy in copies:
        copy.wait()


def body(n_dp, n_sec, n_mp, neighbour_ids, embed_table, enc_gain, kv_weight, queries, grad_out):
    spans, nbr = neighbour_ids.shape
    n_ids = spans * nbr
    owner_rows, enc_width = embed_table.shape
    e_rows, local = kv_weight.shape[1], kv_weight.shape[3]
    heads = local // HEAD_DIM
    tokens = queries.shape[1]
    cap = 3 * n_ids // (2 * n_dp * n_mp)
    nz, n_plane, n_tgt = n_dp // 2, n_sec * n_mp, n_dp // n_sec
    ny = max(1, n_sec // 2)
    half = nz * 32
    nq = 4 if heads % 4 == 0 else 1
    k_long = nz // 2
    cols = heads * HEAD_COLS
    cols = heads * HEAD_COLS
    vmem = pl.BlockSpec(memory_space=pltpu.VMEM)
    dma = pltpu.SemaphoreType.DMA
    out = pl.pallas_call(
        functools.partial(kernel, n_dp, n_sec, n_mp, cap, e_rows),
        out_shape=(
            jax.ShapeDtypeStruct((tokens, local), BF16),
            jax.ShapeDtypeStruct((tokens, local), BF16),
            jax.ShapeDtypeStruct((e_rows, 2, local), BF16),
            jax.ShapeDtypeStruct((n_ids, enc_width), BF16),
        ),
        in_specs=[vmem] * 6,
        out_specs=(vmem,) * 4,
        scratch_shapes=[
            pltpu.VMEM((n_tgt, spans, nbr), jnp.int32),
            pltpu.VMEM((n_tgt, PACK, enc_width), BF16),
            pltpu.VMEM((n_tgt, PACK, enc_width), BF16),
            pltpu.VMEM((ny, n_plane // ny, n_tgt * cap, enc_width), BF16),
            pltpu.VMEM((2 * half, enc_width), BF16),
            pltpu.VMEM((n_ids, n_plane * n_tgt * cap), BF16),
            pltpu.VMEM((n_ids, 2 * half), BF16),
            pltpu.VMEM((2 * half, n_ids), BF16),
            pltpu.VMEM((2 * half, cols), BF16),
            pltpu.VMEM((n_ids, cols), BF16),
            pltpu.VMEM((2 * half, cols), BF16),
            pltpu.VMEM((half, cols), BF16),
            pltpu.VMEM((2, 32, cols), BF16),
            pltpu.VMEM((2, k_long, 32, cols), BF16),
            pltpu.VMEM((4, 32, cols), F32),
            pltpu.VMEM((2, 32, cols), F32),
            pltpu.VMEM((n_ids, enc_width), BF16),
            pltpu.VMEM((spans, n_plane, nbr // n_plane, enc_width), BF16),
            pltpu.VMEM((n_ids, enc_width), BF16),
            dma, dma((n_tgt,)),
            dma((n_tgt,)), dma((n_tgt,)),
            dma((4,)), dma((4,)),
            dma, dma((2, nq, k_long)),
            dma, dma((nq,)),
            dma, dma((nq,)),
            dma((2,)), dma((2, nq, k_long)),
            dma((spans,)), dma((spans,)),
            dma((spans,)), dma((spans,)),
        ],
        compiler_params=pltpu.CompilerParams(
            collective_id=0, has_side_effects=True, vmem_limit_bytes=60 * 1024 * 1024
        ),
        name="layer",
    )(
        neighbour_ids, embed_table, enc_gain, kv_weight[0],
        queries[0], grad_out[0],
    )
    hbm = pl.BlockSpec(memory_space=pl.ANY)
    attn, grad_query, weight_grad, grad_enc = pl.pallas_call(
        settle,
        out_shape=[jax.ShapeDtypeStruct(x.shape, x.dtype) for x in out],
        in_specs=[vmem] * len(out),
        out_specs=[hbm] * len(out),
        scratch_shapes=[dma((len(out),))],
        name="settle",
    )(*out)
    return (
        attn[None],
        grad_query[None],
        weight_grad[None],
        grad_enc.reshape(spans, nbr, enc_width),
    )


def solution(mesh):
    in_specs = (
        P("dp", None),
        P(("dp", "mp"), None),
        P(),
        P("section", "dp", None, "mp"),
        P("section", "dp", "mp"),
        P("section", "dp", "mp"),
    )
    out_specs = (
        P("section", "dp", "mp"),
        P("section", "dp", "mp"),
        P("section", "dp", None, "mp"),
        P("dp", None, None),
    )
    sizes = (mesh.shape["dp"], mesh.shape["section"], mesh.shape["mp"])
    return jax.shard_map(
        functools.partial(body, *sizes), mesh=mesh, in_specs=in_specs, out_specs=out_specs,
        check_vma=False,
    )
```
